512 devices in a mesh: ctx: 64 (over y, z), tp: 8 (over x, core).
Axes of the slice: x: 4, y: 8, z: 8, core: 2. Of those that a mesh axis runs over, the one named last changes fastest.
Arguments:
- queries: bfloat16 [32768, 4096], P('ctx', 'tp'), may hold values from -6 to 6
- key_rows: bfloat16 [32768, 4096], P('ctx', 'tp'), may hold values from -6 to 6
- value_rows: bfloat16 [32768, 4096], P('ctx', 'tp'), may hold values from -6 to 6
- log_decay: float32 [32, 32768], P('tp', 'ctx'), may hold values from -1 to 0
- doc_ids: int32 [32768], P('ctx'), may hold values from 0 to 5, never falling along the last dimension, each value on 1 to 16384 neighbouring positions
- head_gain: float32 [4096], P('tp'), may hold values from 0.1 to 1.9
- out_weight: bfloat16 [4096, 4096], P('ctx', 'tp'), may hold values from -0.09375 to 0.09375
Outputs:
- mixed: bfloat16 [32768, 4096], P('ctx', 'tp')
The draws below stay inside these ranges and needn't reach their ends.
All inputs are finite; a program needn't handle non-finite values.
Results may differ from the reference program's by a relative error of at most 0.013.
Values may be sent and summed in bfloat16 or wider, within the bound.
No kernel may reach another device: no remote copies, remote signals or barrier semaphores. Data moves between devices by JAX's collectives and lax.ppermute only.
A program may use at most 64 MiB of HBM per device.

```python
import math
import jax
import jax.numpy as jnp
import numpy as np
from jax import lax

D = 4096
ATTENTION_PARTS = 32
HD = 128
TOK_DEV = 512
SEQUENCE_SPAN = 32768
BLOCK = 512


def draw_log_decay(key, part):
    key = jax.random.fold_in(key, 11)
    lookup_vectors = jax.random.split(key, 8)
    share = 0.5
    device_blocks = SEQUENCE_SPAN // TOK_DEV
    slow_heads = jax.random.uniform(lookup_vectors[0], (ATTENTION_PARTS,)) < share
    slow_rate = 0.6 / SEQUENCE_SPAN * jnp.exp(jax.random.uniform(lookup_vectors[1], (ATTENTION_PARTS,), jnp.float32, -0.69, 0.69))
    fast_rate = 1.0 / 40.0 * jnp.exp(jax.random.uniform(lookup_vectors[2], (ATTENTION_PARTS,), jnp.float32, -0.69, 0.69))
    forgetting_factor = jnp.where(slow_heads, slow_rate, fast_rate)[:, None]
    per_worker_portion = jnp.exp(jax.random.uniform(lookup_vectors[3], (ATTENTION_PARTS, device_blocks), jnp.float32, -0.7, 0.7))
    paused_blocks = jax.random.uniform(lookup_vectors[7], (ATTENTION_PARTS, device_blocks)) < 0.5
    per_worker_portion = per_worker_portion * jnp.where(paused_blocks, 0.005, 1.0)
    per_worker_portion = jnp.repeat(per_worker_portion, TOK_DEV, axis=1)
    approximate_guess = jax.random.uniform(lookup_vectors[4], (ATTENTION_PARTS, SEQUENCE_SPAN), jnp.float32, 0.5, 1.5)
    segment_runs = jax.random.uniform(lookup_vectors[5], (ATTENTION_PARTS, SEQUENCE_SPAN)) < 2.0 / SEQUENCE_SPAN
    fitting_objective = jax.random.uniform(lookup_vectors[6], (ATTENTION_PARTS, SEQUENCE_SPAN), jnp.float32, math.log(0.5), math.log(0.8))
    return (-forgetting_factor * per_worker_portion * approximate_guess + jnp.where(segment_runs, fitting_objective, 0.0)).astype(jnp.float32)


def shard_levels(own_key, dims, cuts, low, top_value):
    factor_of = 1.0
    for axis_at, blocks in cuts:
        heights = jax.random.uniform(jax.random.fold_in(jax.random.fold_in(own_key, 6), axis_at), (blocks,), jnp.float32, low / len(cuts), top_value / len(cuts))
        factor_of = factor_of * jnp.repeat(jnp.exp(heights), dims[axis_at] // blocks).reshape((-1,) + (1,) * (len(dims) - 1 - axis_at))
    return factor_of


def split_up(amount, total, most, lean):
    weights = [(1 << 20) // math.isqrt(rank ** lean) + 1 for rank in range(2, amount + 1)]
    surplus, given = total - most - (amount - 1), [1] * (amount - 1)
    while surplus > 0:
        movable = [i for i in range(amount - 1) if given[i] < most]
        whole, left = sum([weights[i] for i in movable]), surplus
        for i in movable:
            more = min(most - given[i], max(1, left * weights[i] // whole), surplus)
            given[i] = given[i] + more
            surplus = surplus - more
    return np.array([most] + given)


def ragged_sizes(stream_key, number_of, total, most, slope):
    if number_of == 2:
        one = jax.random.randint(stream_key, (), max(1, total - most), min(most, total - 1) + 1)
        return jnp.stack([one, total - one])
    lengths = jnp.asarray(split_up(number_of, total, most, slope), jnp.int32)
    twos = (number_of - 1) // 2
    source_of, sink = lengths[1:1 + 2 * twos:2], lengths[2:2 + 2 * twos:2]
    margin = jnp.minimum(source_of - 1, most - sink)
    shifted = jax.random.randint(jax.random.fold_in(stream_key, 1), (twos,), 0, 1 << 20) % (margin + 1)
    lengths = lengths.at[1:1 + 2 * twos:2].set(source_of - shifted).at[2:2 + 2 * twos:2].set(sink + shifted)
    return lengths[jax.random.permutation(jax.random.fold_in(stream_key, 2), number_of)]


def noise(rng, extent, width, most, cuts=(), held_as=jnp.bfloat16):
    factor_of = shard_levels(rng, extent, cuts, -0.22, 0.18) if cuts else 1.0
    values = jax.random.normal(rng, extent, jnp.float32) * width * factor_of
    return jnp.minimum(jnp.maximum(values, -most), most).astype(held_as)


def setup_inputs(seed: int = 0) -> dict:
    streams_of = jax.random.split(jax.random.key(seed), 8)
    return {
        "queries": noise(streams_of[0], (SEQUENCE_SPAN, D), 1.0, 6.0, ((0, 64), (1, 8))),
        "key_rows": noise(streams_of[1], (SEQUENCE_SPAN, D), 1.0, 6.0, ((0, 64), (1, 8))),
        "value_rows": noise(streams_of[2], (SEQUENCE_SPAN, D), 1.0, 6.0, ((0, 64), (1, 8))),
        "log_decay": draw_log_decay(jax.random.fold_in(streams_of[7], 71), 0),
        "doc_ids": jnp.searchsorted(jnp.cumsum(ragged_sizes(streams_of[4], 6, SEQUENCE_SPAN, SEQUENCE_SPAN // 2, 0)), jnp.arange(SEQUENCE_SPAN), side="right").astype(jnp.int32),
        "head_gain": jnp.clip(1.0 + 0.18 * jax.random.normal(streams_of[5], (D,), jnp.float32), 0.1, 1.9),
        "out_weight": noise(streams_of[6], (D, D), D ** -0.5, 0.09375, ((0, 64), (1, 8))),
    }


def mix_block(carry_in, pieces):
    memory, prior_doc = carry_in
    query_blk, key_blk, value_blk, log_block, doc_block = pieces
    query_wide = query_blk.astype(jnp.float32)
    key_wide = key_blk.astype(jnp.float32)
    value_wide = value_blk.astype(jnp.float32)
    cumulative = jnp.cumsum(log_block, axis=1)
    positions = jnp.arange(doc_block.shape[0])
    causal = positions[:, None] >= positions[None, :]
    same_doc = jnp.logical_and(doc_block[:, None] == doc_block[None, :], causal)[None]
    log_gap = cumulative[:, :, None] - cumulative[:, None, :]
    decay_mask = jnp.where(same_doc, jnp.exp(jnp.where(same_doc, log_gap, 0.0)), 0.0)
    scores = jnp.einsum('thd,shd->hts', query_wide, key_wide, precision=lax.Precision.HIGHEST)
    weighted = (scores * decay_mask).astype(jnp.bfloat16)
    local_part = jnp.einsum('hts,shd->thd', weighted.astype(jnp.float32), value_wide, precision=lax.Precision.HIGHEST)
    linked = (doc_block == prior_doc).astype(jnp.float32)
    reach_in = jnp.exp(cumulative).T * linked[:, None]
    carried = jnp.einsum('thd,hde->the', query_wide, memory, precision=lax.Precision.HIGHEST)
    heads_out = local_part + reach_in[:, :, None] * carried
    final_log = cumulative[:, -1]
    to_end = jnp.exp(final_log[:, None] - cumulative) * (doc_block == doc_block[-1]).astype(jnp.float32)[None, :]
    decayed = (key_wide * to_end.T[:, :, None]).astype(jnp.bfloat16)
    retain = jnp.exp(final_log) * jnp.all(doc_block == prior_doc).astype(jnp.float32)
    update = jnp.einsum('shd,she->hde', decayed.astype(jnp.float32), value_wide, precision=lax.Precision.HIGHEST)
    memory = retain[:, None, None] * memory + update
    return ((memory, doc_block[-1]), heads_out)

def finish(heads_out, head_gain):
    scale = lax.rsqrt(lax.optimization_barrier(jnp.mean(heads_out * heads_out, axis=-1, keepdims=True)) + 1e-06)
    flat = (heads_out * scale).reshape(heads_out.shape[0], -1)
    return (flat * head_gain[None, :]).astype(jnp.bfloat16)

def reference(queries, key_rows, value_rows, log_decay, doc_ids, head_gain, out_weight):
    blocks = SEQUENCE_SPAN // BLOCK

    def split(rows_in):
        return rows_in.reshape(blocks, BLOCK, ATTENTION_PARTS, HD)
    log_blocks = log_decay.reshape(ATTENTION_PARTS, blocks, BLOCK).transpose(1, 0, 2)
    doc_blocks = doc_ids.reshape(blocks, BLOCK)
    start = (jnp.zeros((ATTENTION_PARTS, HD, HD), jnp.float32), doc_ids[0])
    _, heads_out = lax.scan(mix_block, start, (split(queries), split(key_rows), split(value_rows), log_blocks, doc_blocks))
    heads_out = heads_out.reshape(SEQUENCE_SPAN, ATTENTION_PARTS, HD)
    normed = finish(heads_out, head_gain)
    return jnp.dot(normed, out_weight, preferred_element_type=jnp.float32).astype(jnp.bfloat16)
```

```python
import jax
import jax.numpy as jnp
from jax import lax
from jax.experimental import pallas as pl
from jax.experimental.pallas import tpu as pltpu
from jax.sharding import Mesh, PartitionSpec as P

HD = 128
BLOCK = 512
HEADS = 4
RING = 8
SLICE = HEADS * HD // RING
ROWS = SLICE + 16
ALL = ("y", "z", "x", "c")
NT = (((1,), (1,)), ((), ()))
TN = (((0,), (0,)), ((), ()))
VMEM = pl.BlockSpec(memory_space=pltpu.VMEM)
SMEM = pl.BlockSpec(memory_space=pltpu.SMEM)


def flat_pairs(sizes, move):
    ny, nz, nx, nc = sizes
    index = lambda y, z, x, c: (((y % ny) * nz + z % nz) * nx + x % nx) * nc + c % nc
    return [
        (index(y, z, x, c), index(*move(y, z, x, c)))
        for y in range(ny)
        for z in range(nz)
        for x in range(nx)
        for c in range(nc)
    ]


def parts_of(value):
    high = value.astype(jnp.bfloat16)
    rest = value - high.astype(jnp.float32)
    middle = rest.astype(jnp.bfloat16)
    low = (rest - middle.astype(jnp.float32)).astype(jnp.bfloat16)
    return high, middle, low


def dot(a, b, dims=(((1,), (0,)), ((), ()))):
    return lax.dot_general(a, b, dims, preferred_element_type=jnp.float32)


def running(log_ref, doc_ref, stage):
    docs = doc_ref[...].astype(jnp.float32)
    lane = lax.broadcasted_iota(jnp.int32, docs.shape, 1)
    stage[...] = jnp.zeros_like(stage)
    stage[0:HEADS, :] = log_ref[...]
    stage[HEADS : HEADS + 1, :] = docs - jnp.where(lane == 0, 0.0, pltpu.roll(docs, 1, 1))
    parts = parts_of(stage[...])
    row = lax.broadcasted_iota(jnp.int32, (BLOCK, BLOCK), 0)
    column = lax.broadcasted_iota(jnp.int32, (BLOCK, BLOCK), 1)
    lower = jnp.where(row >= column, 1.0, 0.0).astype(jnp.bfloat16)
    down = sum(dot(lower, part, NT) for part in parts)
    return parts, lower, down


def state_kernel(key_ref, value_ref, log_ref, doc_ref, out_ref, stage):
    _, _, down = running(log_ref, doc_ref, stage)
    final = down[BLOCK - 1 : BLOCK, :]
    kept = down[:, HEADS : HEADS + 1] == final[:, HEADS : HEADS + 1]
    to_end = jnp.where(kept, jnp.exp(final - down), 0.0)
    meta_row = lax.broadcasted_iota(jnp.int32, (16, HD), 0)
    for h in range(HEADS):
        span = slice(h * HD, (h + 1) * HD)
        decayed = (key_ref[:, span].astype(jnp.float32) * to_end[:, h : h + 1]).astype(jnp.bfloat16)
        state = dot(decayed, value_ref[:, span], TN).astype(jnp.bfloat16)
        high, middle, low = [part.astype(jnp.float32) for part in parts_of(final[:, h : h + 1])]
        meta = jnp.where(meta_row == 0, high, jnp.where(meta_row == 1, middle, jnp.where(meta_row == 2, low, 0.0)))
        meta = jnp.where(meta_row == 3, final[:, HEADS : HEADS + 1], meta).astype(jnp.bfloat16)
        for half in range(2):
            out_ref[2 * h + half, 0:SLICE, :] = state[half * SLICE : (half + 1) * SLICE]
            out_ref[2 * h + half, SLICE:ROWS, :] = meta


def read_meta(ref, k):
    meta = ref[k, SLICE:ROWS, :].astype(jnp.float32)
    return meta[0:1] + meta[1:2] + meta[2:3], meta[3:4]


def row_kernel(states_ref, out_ref):
    total = jnp.zeros((SLICE, HD), jnp.float32)
    logs = jnp.zeros((1, HD), jnp.float32)
    prior = None
    for k in range(RING):
        log, last = read_meta(states_ref, k)
        if k:
            total = total * jnp.where(last == prior, jnp.exp(log), 0.0)
        total = total + states_ref[k, 0:SLICE, :].astype(jnp.float32)
        logs = logs + log
        prior = last
    meta_row = lax.broadcasted_iota(jnp.int32, (16, HD), 0)
    high, middle, low = [part.astype(jnp.float32) for part in parts_of(logs)]
    meta = jnp.where(meta_row == 0, high, jnp.where(meta_row == 1, middle, jnp.where(meta_row == 2, low, 0.0)))
    meta = jnp.where(meta_row == 3, prior, meta).astype(jnp.bfloat16)
    total = total.astype(jnp.bfloat16)
    for k in range(RING):
        out_ref[k, 0:SLICE, :] = total
        out_ref[k, SLICE:ROWS, :] = meta


def enter_kernel(place_ref, states_ref, rows_ref, out_ref):
    here = place_ref[0]
    running_state = jnp.zeros((SLICE, HD), jnp.float32)
    memory = running_state
    prior = jnp.zeros((1, HD), jnp.float32)
    prior_row = prior
    for k in range(RING):
        log, last = read_meta(rows_ref, k)
        memory = jnp.where(here == k, running_state, memory)
        prior = jnp.where(here == k, prior_row, prior)
        running_state = running_state * jnp.where(last == prior_row, jnp.exp(log), 0.0)
        running_state = running_state + rows_ref[k, 0:SLICE, :].astype(jnp.float32)
        prior_row = last
    for k in range(RING):
        out_ref[k, 0:SLICE, :] = memory.astype(jnp.bfloat16)
        out_ref[k, SLICE:ROWS, :] = jnp.broadcast_to(prior, (16, HD)).astype(jnp.bfloat16)
        log, last = read_meta(states_ref, k)
        memory = memory * jnp.where(last == prior, jnp.exp(log), 0.0)
        memory = memory + states_ref[k, 0:SLICE, :].astype(jnp.float32)
        prior = last


def attend_kernel(query_ref, key_ref, value_ref, log_ref, doc_ref, memory_ref, gain_ref, out_ref, stage, mask):
    parts, lower, down = running(log_ref, doc_ref, stage)
    across = sum(dot(part, lower, NT) for part in parts)
    doc_down = down[:, HEADS : HEADS + 1]
    mask[...] = jnp.where(doc_down == across[HEADS : HEADS + 1, :], 0.0, -1e30)
    row = lax.broadcasted_iota(jnp.int32, (BLOCK, BLOCK), 0)
    column = lax.broadcasted_iota(jnp.int32, (BLOCK, BLOCK), 1)
    mask[...] = jnp.where(row >= column, mask[...], -1e30)
    prior = memory_ref[0, SLICE : SLICE + 16, :].astype(jnp.float32)[0:1, 0:1]
    reach = jnp.where(doc_down == prior, jnp.exp(down), 0.0)
    part_rows = BLOCK // 2
    for h in range(HEADS):
        span = slice(h * HD, (h + 1) * HD)
        memory = jnp.concatenate([memory_ref[2 * h, 0:SLICE, :], memory_ref[2 * h + 1, 0:SLICE, :]], axis=0)
        for i in range(2):
            rows = slice(i * part_rows, (i + 1) * part_rows)
            seen = slice(0, (i + 1) * part_rows)
            query = query_ref[rows, span]
            scores = dot(query, key_ref[seen, span], NT)
            gap = down[rows, h : h + 1] - across[h : h + 1, seen] + mask[rows, seen]
            weighted = (scores * jnp.exp(gap)).astype(jnp.bfloat16)
            heads = dot(weighted, value_ref[seen, span])
            heads = heads + reach[rows, h : h + 1] * dot(query, memory)
            scale = lax.rsqrt(jnp.mean(heads * heads, axis=-1, keepdims=True) + 1e-06)
            out_ref[rows, span] = (heads * scale * gain_ref[:, span]).astype(jnp.bfloat16)


def project_kernel(places_ref, own_ref, before_ref, after_ref, far_one_ref, far_two_ref, weight_ref, out_ref):
    step = pl.program_id(0)
    half = BLOCK // 2

    @pl.when(step == 0)
    def _():
        out_ref[...] = dot(own_ref[...], weight_ref[0])

    @pl.when(step == 1)
    def _():
        out_ref[...] += dot(before_ref[...], weight_ref[0])

    @pl.when(step == 2)
    def _():
        out_ref[...] += dot(after_ref[...], weight_ref[0])

    @pl.when(step == 3)
    def _():
        out_ref[0:half, :] += dot(far_one_ref[...], weight_ref[0])
        out_ref[half:BLOCK, :] += dot(far_two_ref[...], weight_ref[0])


def project(places, blocks, weight):
    columns = weight.shape[-1]
    whole = lambda array: pl.BlockSpec(array.shape, lambda k, places: (0, 0))
    return pl.pallas_call(
        project_kernel,
        out_shape=jax.ShapeDtypeStruct((BLOCK, columns), jnp.float32),
        grid_spec=pltpu.PrefetchScalarGridSpec(
            num_scalar_prefetch=1,
            grid=(4,),
            in_specs=[whole(block) for block in blocks]
            + [pl.BlockSpec((1, BLOCK, columns), lambda k, places: (places[k], 0, 0))],
            out_specs=pl.BlockSpec((BLOCK, columns), lambda k, places: (0, 0)),
        ),
        compiler_params=pltpu.CompilerParams(vmem_limit_bytes=32 * 2**20),
        cost_estimate=pl.CostEstimate(
            flops=2 * BLOCK * 4 * BLOCK * columns, bytes_accessed=6 * 2**20, transcendentals=0
        ),
    )(places, *blocks, weight)


def call(kernel, out_shape, args, specs, scratch=(), flops=0, transcendentals=0):
    return pl.pallas_call(
        kernel,
        out_shape=out_shape,
        in_specs=specs,
        out_specs=VMEM,
        scratch_shapes=list(scratch),
        compiler_params=pltpu.CompilerParams(vmem_limit_bytes=32 * 2**20),
        cost_estimate=pl.CostEstimate(flops=flops, bytes_accessed=2**20, transcendentals=transcendentals),
    )(*args)


def local(sizes, queries, key_rows, value_rows, log_decay, doc_ids, head_gain, out_weight):
    nx = sizes[2]
    y, x, c = (lax.axis_index(name) for name in ("y", "x", "c"))
    slices = jax.ShapeDtypeStruct((RING, ROWS, HD), jnp.bfloat16)
    docs = doc_ids.reshape(1, BLOCK)
    stage = pltpu.VMEM((8, BLOCK), jnp.float32)

    swap = flat_pairs(
        sizes, lambda y, z, x, c: (y, z, x, c) if y % 2 == c else (y + 1 if c else y - 1, z, x, 1 - c)
    )
    weight = lax.all_gather(lax.ppermute(out_weight, ALL, swap), ("y", "z"), axis=0, tiled=True)
    weight = weight.reshape(8, BLOCK, -1)

    states = call(
        state_kernel, slices, (key_rows, value_rows, log_decay, docs), [VMEM] * 4, [stage], 10**8, 4096
    )
    states = lax.all_to_all(states, "z", 0, 0, tiled=True)
    rows = call(row_kernel, slices, (states,), [VMEM])
    rows = lax.all_to_all(rows, "y", 0, 0, tiled=True)
    entering = call(enter_kernel, slices, (y.reshape(1), states, rows), [SMEM, VMEM, VMEM])
    entering = lax.all_to_all(entering, "z", 0, 0, tiled=True)
    normed = call(
        attend_kernel,
        jax.ShapeDtypeStruct(queries.shape, jnp.bfloat16),
        (queries, key_rows, value_rows, log_decay, docs, entering, head_gain.reshape(1, -1)),
        [VMEM] * 7,
        [stage, pltpu.VMEM((BLOCK, BLOCK), jnp.float32)],
        10**9,
        2**20,
    )

    right = [(i, (i + 1) % nx) for i in range(nx)]
    left = [(i, (i - 1) % nx) for i in range(nx)]
    before = lax.ppermute(normed, "x", right)
    after = lax.ppermute(normed, "x", left)
    half = BLOCK // 2
    far_one = lax.ppermute(before[:half], "x", right)
    far_two = lax.ppermute(after[half:], "x", left)
    blocks = (normed, before, after, far_one, far_two)
    order = jnp.stack([x, (x + nx - 1) % nx, (x + 1) % nx, (x + 2) % nx])
    other = project(2 * order + 1 - c, blocks, weight)
    other = lax.ppermute(other, "c", [(0, 1), (1, 0)])
    own = project(2 * order + c, blocks, weight)
    return (own + other).astype(jnp.bfloat16)


def solution(mesh):
    sizes = (8, 8, 4, 2)
    split = Mesh(mesh.devices.reshape(sizes), ALL)
    ctx, tp = ("y", "z"), ("x", "c")
    return jax.shard_map(
        lambda *args: local(sizes, *args),
        mesh=split,
        in_specs=(P(ctx, tp), P(ctx, tp), P(ctx, tp), P(tp, ctx), P(ctx), P(tp), P(ctx, tp)),
        out_specs=P(ctx, tp),
        check_vma=False,
    )
```

```python
import jax
import jax.numpy as jnp
from jax import lax
from jax.experimental import pallas as pl
from jax.experimental.pallas import tpu as pltpu
from jax.sharding import Mesh, PartitionSpec as P

HD = 128
BLOCK = 512
HEADS = 4
RING = 8
SLICE = HEADS * HD // RING
ROWS = SLICE + 16
FULL = ROWS + 4 * 64
ALL = ("y", "z", "x", "c")
NT = (((1,), (1,)), ((), ()))
TN = (((0,), (0,)), ((), ()))
VMEM = pl.BlockSpec(memory_space=pltpu.VMEM)
ANY = pl.BlockSpec(memory_space=pl.ANY)
SMEM = pl.BlockSpec(memory_space=pltpu.SMEM)


def flat_pairs(sizes, move):
    ny, nz, nx, nc = sizes
    index = lambda y, z, x, c: (((y % ny) * nz + z % nz) * nx + x % nx) * nc + c % nc
    return [
        (index(y, z, x, c), index(*move(y, z, x, c)))
        for y in range(ny)
        for z in range(nz)
        for x in range(nx)
        for c in range(nc)
    ]


def parts_of(value):
    high = value.astype(jnp.bfloat16)
    rest = value - high.astype(jnp.float32)
    middle = rest.astype(jnp.bfloat16)
    low = (rest - middle.astype(jnp.float32)).astype(jnp.bfloat16)
    return high, middle, low


def dot(a, b, dims=(((1,), (0,)), ((), ()))):
    return lax.dot_general(a, b, dims, preferred_element_type=jnp.float32)


def running(log, doc, stage):
    docs = doc.astype(jnp.float32)
    lane = lax.broadcasted_iota(jnp.int32, docs.shape, 1)
    stage[...] = jnp.zeros_like(stage)
    stage[0:HEADS, :] = log
    stage[HEADS : HEADS + 1, :] = docs - jnp.where(lane == 0, 0.0, pltpu.roll(docs, 1, 1))
    parts = parts_of(stage[...])
    row = lax.broadcasted_iota(jnp.int32, (BLOCK, BLOCK), 0)
    column = lax.broadcasted_iota(jnp.int32, (BLOCK, BLOCK), 1)
    lower = jnp.where(row >= column, 1.0, 0.0).astype(jnp.bfloat16)
    down = sum(dot(lower, part, NT) for part in parts)
    return parts, lower, down


def fetch(sources, targets, sems):
    copies = [pltpu.make_async_copy(s, t, sems.at[i]) for i, (s, t) in enumerate(zip(sources, targets))]
    for copy in copies:
        copy.start()
    return copies


def meta_of(log, last):
    row = lax.broadcasted_iota(jnp.int32, (16, HD), 0)
    high, middle, low = [part.astype(jnp.float32) for part in parts_of(log)]
    meta = jnp.where(row == 0, high, jnp.where(row == 1, middle, jnp.where(row == 2, low, 0.0)))
    return jnp.where(row == 3, last, meta).astype(jnp.bfloat16)


def read_meta(meta):
    meta = meta.astype(jnp.float32)
    return meta[0:1] + meta[1:2] + meta[2:3], meta[3:4]


def state_kernel(log_in, doc_in, key_in, value_in, weight_in, out_ref, log, doc, key, value, weight, stage, sems):
    copies = fetch(
        (log_in, doc_in, key_in, value_in, weight_in), (log, doc, key, value, weight), sems
    )
    copies[0].wait()
    copies[1].wait()
    _, _, down = running(log[...], doc[...], stage)
    final = down[BLOCK - 1 : BLOCK, :]
    kept = down[:, HEADS : HEADS + 1] == final[:, HEADS : HEADS + 1]
    to_end = jnp.where(kept, jnp.exp(final - down), 0.0)
    copies[2].wait()
    copies[3].wait()
    for h in range(HEADS):
        span = slice(h * HD, (h + 1) * HD)
        decayed = (key[:, span].astype(jnp.float32) * to_end[:, h : h + 1]).astype(jnp.bfloat16)
        state = dot(decayed, value[:, span], TN).astype(jnp.bfloat16)
        meta = meta_of(final[:, h : h + 1], final[:, HEADS : HEADS + 1])
        for half in range(2):
            out_ref[2 * h + half, 0:SLICE, :] = state[half * SLICE : (half + 1) * SLICE]
            out_ref[2 * h + half, SLICE:ROWS, :] = meta
    copies[4].wait()
    for k in range(RING):
        for j in range(4):
            out_ref[k, ROWS + 64 * j : ROWS + 64 * (j + 1), :] = weight[:, j * HD : (j + 1) * HD]


def row_kernel(states_ref, out_ref, weight_ref):
    total = jnp.zeros((SLICE, HD), jnp.float32)
    logs = jnp.zeros((1, HD), jnp.float32)
    prior = None
    for k in range(RING):
        log, last = read_meta(states_ref[k, SLICE:ROWS, :])
        if k:
            total = total * jnp.where(last == prior, jnp.exp(log), 0.0)
        total = total + states_ref[k, 0:SLICE, :].astype(jnp.float32)
        logs = logs + log
        prior = last
    out_ref[0:SLICE, :] = total.astype(jnp.bfloat16)
    out_ref[SLICE:ROWS, :] = meta_of(logs, prior)
    weight_ref[...] = states_ref[:, ROWS:FULL, :]


def join_kernel(later_ref, earlier_ref, out_ref):
    log, last = read_meta(later_ref[SLICE:ROWS, :])
    log_before, last_before = read_meta(earlier_ref[SLICE:ROWS, :])
    keep = jnp.where(last == last_before, jnp.exp(log), 0.0)
    total = later_ref[0:SLICE, :].astype(jnp.float32) + keep * earlier_ref[0:SLICE, :].astype(jnp.float32)
    out_ref[0:SLICE, :] = total.astype(jnp.bfloat16)
    out_ref[SLICE:ROWS, :] = meta_of(log + log_before, last)


def enter_kernel(states_ref, rows_ref, out_ref):
    memory = rows_ref[0:SLICE, :].astype(jnp.float32)
    _, prior = read_meta(rows_ref[SLICE:ROWS, :])
    for k in range(RING):
        out_ref[k, 0:SLICE, :] = memory.astype(jnp.bfloat16)
        out_ref[k, SLICE:ROWS, :] = jnp.broadcast_to(prior, (16, HD)).astype(jnp.bfloat16)
        log, last = read_meta(states_ref[k, SLICE:ROWS, :])
        memory = memory * jnp.where(last == prior, jnp.exp(log), 0.0)
        memory = memory + states_ref[k, 0:SLICE, :].astype(jnp.float32)
        prior = last


def attend_kernel(
    log_in, doc_in, query_in, key_in, value_in, gain_in, memory_ref, out_ref,
    log, doc, query_ref, key_ref, value_ref, gain_ref, stage, mask, sems,
):
    copies = fetch(
        (log_in, doc_in, query_in, key_in, value_in, gain_in),
        (log, doc, query_ref, key_ref, value_ref, gain_ref),
        sems,
    )
    copies[0].wait()
    copies[1].wait()
    parts, lower, down = running(log[...], doc[...], stage)
    across = sum(dot(part, lower, NT) for part in parts)
    doc_down = down[:, HEADS : HEADS + 1]
    mask[...] = jnp.where(doc_down == across[HEADS : HEADS + 1, :], 0.0, -1e30)
    row = lax.broadcasted_iota(jnp.int32, (BLOCK, BLOCK), 0)
    column = lax.broadcasted_iota(jnp.int32, (BLOCK, BLOCK), 1)
    mask[...] = jnp.where(row >= column, mask[...], -1e30)
    prior = memory_ref[0, SLICE : SLICE + 16, :].astype(jnp.float32)[0:1, 0:1]
    reach = jnp.where(doc_down == prior, jnp.exp(down), 0.0)
    part_rows = BLOCK // 2
    for copy in copies[2:]:
        copy.wait()
    for h in range(HEADS):
        span = slice(h * HD, (h + 1) * HD)
        memory = jnp.concatenate([memory_ref[2 * h, 0:SLICE, :], memory_ref[2 * h + 1, 0:SLICE, :]], axis=0)
        for i in range(2):
            rows = slice(i * part_rows, (i + 1) * part_rows)
            seen = slice(0, (i + 1) * part_rows)
            query = query_ref[rows, span]
            scores = dot(query, key_ref[seen, span], NT)
            gap = down[rows, h : h + 1] - across[h : h + 1, seen] + mask[rows, seen]
            weighted = (scores * jnp.exp(gap)).astype(jnp.bfloat16)
            heads = dot(weighted, value_ref[seen, span])
            heads = heads + reach[rows, h : h + 1] * dot(query, memory)
            scale = lax.rsqrt(jnp.mean(heads * heads, axis=-1, keepdims=True) + 1e-06)
            out_ref[rows, span] = (heads * scale * gain_ref[:, span]).astype(jnp.bfloat16)


def project_kernel(places_ref, *refs):
    blocks, weights, (out_ref, held, sems) = refs[:5], refs[5:13], refs[13:]
    half = BLOCK // 2
    for s in range(4):
        for d in range(RING):

            @pl.when(places_ref[s] == d)
            def _():
                pltpu.make_async_copy(weights[d], held.at[s], sems.at[s]).start()

    for s in range(4):
        pltpu.make_async_copy(weights[0], held.at[s], sems.at[s]).wait()
        weight = jnp.concatenate(
            [held[s, :, 64 * j : 64 * (j + 1), :].reshape(BLOCK, HD) for j in range(4)], axis=1
        )
        if s == 0:
            out_ref[...] = dot(blocks[0][...], weight)
        elif s < 3:
            out_ref[...] += dot(blocks[s][...], weight)
        else:
            out_ref[0:half, :] += dot(blocks[3][...], weight)
            out_ref[half:BLOCK, :] += dot(blocks[4][...], weight)


def call(kernel, out_shape, args, specs, scratch=(), flops=0, transcendentals=0):
    return pl.pallas_call(
        kernel,
        out_shape=out_shape,
        in_specs=specs,
        out_specs=jax.tree.map(lambda _: VMEM, out_shape),
        scratch_shapes=list(scratch),
        compiler_params=pltpu.CompilerParams(vmem_limit_bytes=24 * 2**20),
        cost_estimate=pl.CostEstimate(flops=flops, bytes_accessed=2**20, transcendentals=transcendentals),
    )(*args)


def local(sizes, queries, key_rows, value_rows, log_decay, doc_ids, head_gain, out_weight):
    ny, _, nx, _ = sizes
    y, x, c = (lax.axis_index(name) for name in ("y", "x", "c"))
    shape = lambda *dims: jax.ShapeDtypeStruct(dims, jnp.bfloat16)
    docs, gains = doc_ids.reshape(1, BLOCK), head_gain.reshape(1, -1)
    wide = pltpu.VMEM(queries.shape, jnp.bfloat16)
    logs_held = pltpu.VMEM(log_decay.shape, jnp.float32)
    docs_held = pltpu.VMEM(docs.shape, jnp.int32)
    stage = pltpu.VMEM((8, BLOCK), jnp.float32)

    swap = flat_pairs(
        sizes, lambda y, z, x, c: (y, z, x, c) if y % 2 == c else (y + 1 if c else y - 1, z, x, 1 - c)
    )
    weight = lax.ppermute(out_weight, ALL, swap)

    states = call(
        state_kernel,
        shape(RING, FULL, HD),
        (log_decay, docs, key_rows, value_rows, weight),
        [ANY] * 5,
        [logs_held, docs_held, wide, wide, pltpu.VMEM(weight.shape, jnp.bfloat16), stage, pltpu.SemaphoreType.DMA((5,))],
        10**8,
        4096,
    )
    states = lax.all_to_all(states, "z", 0, 0, tiled=True)
    rows, weight = call(row_kernel, (shape(ROWS, HD), shape(RING, 256, HD)), (states,), [VMEM])

    up = lambda value, steps: lax.ppermute(value, "y", [(i, i + steps) for i in range(ny - steps)])
    right = [(i, (i + 1) % ny) for i in range(ny)]
    left = [(i, (i - 1) % ny) for i in range(ny)]
    rows = call(join_kernel, shape(ROWS, HD), (rows, up(rows, 1)), [VMEM] * 2)
    rows = call(join_kernel, shape(ROWS, HD), (rows, up(rows, 2)), [VMEM] * 2)
    rows = up(rows, 1)
    weights = {0: weight}
    for step in range(1, 5):
        weights[-step % RING] = lax.ppermute(weights[(1 - step) % RING], "y", right)
        if step < 4:
            weights[step] = lax.ppermute(weights[step - 1], "y", left)

    entering = call(enter_kernel, shape(RING, ROWS, HD), (states, rows), [VMEM] * 2)
    entering = lax.all_to_all(entering, "z", 0, 0, tiled=True)
    normed = call(
        attend_kernel,
        shape(*queries.shape),
        (log_decay, docs, queries, key_rows, value_rows, gains, entering),
        [ANY] * 6 + [VMEM],
        [logs_held, docs_held, wide, wide, wide, pltpu.VMEM(gains.shape, jnp.float32), stage]
        + [pltpu.VMEM((BLOCK, BLOCK), jnp.float32), pltpu.SemaphoreType.DMA((6,))],
        10**9,
        2**20,
    )

    right = [(i, (i + 1) % nx) for i in range(nx)]
    left = [(i, (i - 1) % nx) for i in range(nx)]
    before = lax.ppermute(normed, "x", right)
    after = lax.ppermute(normed, "x", left)
    half = BLOCK // 2
    far_one = lax.ppermute(before[:half], "x", right)
    far_two = lax.ppermute(after[half:], "x", left)
    blocks = [normed, before, after, far_one, far_two]
    order = jnp.stack([x, (x + nx - 1) % nx, (x + 1) % nx, (x + 2) % nx])
    project = lambda core: call(
        project_kernel,
        jax.ShapeDtypeStruct(queries.shape, jnp.float32),
        ((2 * order + core - y) % ny, *blocks, *(weights[d] for d in range(RING))),
        [SMEM] + [VMEM] * 5 + [ANY] * RING,
        [pltpu.VMEM((4, RING, 256, HD), jnp.bfloat16), pltpu.SemaphoreType.DMA((4,))],
        2 * 10**9,
    )
    other = lax.ppermute(project(1 - c), "c", [(0, 1), (1, 0)])
    return (project(c) + other).astype(jnp.bfloat16)


def solution(mesh):
    sizes = (8, 8, 4, 2)
    split = Mesh(mesh.devices.reshape(sizes), ALL)
    ctx, tp = ("y", "z"), ("x", "c")
    return jax.shard_map(
        lambda *args: local(sizes, *args),
        mesh=split,
        in_specs=(P(ctx, tp), P(ctx, tp), P(ctx, tp), P(tp, ctx), P(ctx), P(tp), P(ctx, tp)),
        out_specs=P(ctx, tp),
        check_vma=False,
    )
```

```python
import jax
import jax.numpy as jnp
from jax import lax
from jax.experimental import pallas as pl
from jax.experimental.pallas import tpu as pltpu
from jax.sharding import Mesh, PartitionSpec as P

HD = 128
BLOCK = 512
HEADS = 4
RING = 8
SLICE = HEADS * HD // RING
ROWS = SLICE + 16
GRANT = 62
FULL = ROWS + 4 * 64
ALL = ("y", "z", "x", "c")
NT = (((1,), (1,)), ((), ()))
TN = (((0,), (0,)), ((), ()))
VMEM = pl.BlockSpec(memory_space=pltpu.VMEM)
ANY = pl.BlockSpec(memory_space=pl.ANY)
SMEM = pl.BlockSpec(memory_space=pltpu.SMEM)


def parts_of(value):
    high = value.astype(jnp.bfloat16)
    rest = value - high.astype(jnp.float32)
    middle = rest.astype(jnp.bfloat16)
    low = (rest - middle.astype(jnp.float32)).astype(jnp.bfloat16)
    return high, middle, low


def dot(a, b, dims=(((1,), (0,)), ((), ()))):
    return lax.dot_general(a, b, dims, preferred_element_type=jnp.float32)


def running(log, doc, stage):
    stage[...] = jnp.zeros_like(stage)
    stage[0:HEADS, :] = log
    total = stage[...]
    lane = lax.broadcasted_iota(jnp.int32, total.shape, 1)
    step = 1
    while step < BLOCK:
        total = total + jnp.where(lane >= step, pltpu.roll(total, step, 1), 0.0)
        step *= 2
    stage[0:HEADS, :] = total[0:HEADS, :]
    stage[HEADS : HEADS + 1, :] = doc.astype(jnp.float32)
    across = stage[...]
    return across, jnp.transpose(across)


def fetch(sources, targets, sems):
    copies = [pltpu.make_async_copy(s, t, sems.at[i]) for i, (s, t) in enumerate(zip(sources, targets))]
    for copy in copies:
        copy.start()
    return copies


def meta_of(log, last):
    row = lax.broadcasted_iota(jnp.int32, (16, HD), 0)
    high, middle, low = [part.astype(jnp.float32) for part in parts_of(log)]
    meta = jnp.where(row == 0, high, jnp.where(row == 1, middle, jnp.where(row == 2, low, 0.0)))
    return jnp.where(row == 3, last, meta).astype(jnp.bfloat16)


def read_meta(meta):
    meta = meta.astype(jnp.float32)
    return meta[0:1] + meta[1:2] + meta[2:3], meta[3:4]


def state_kernel(log_in, doc_in, key_in, value_in, weight_in, out_ref, log, doc, key, value, weight, stage, sems):
    copies = fetch(
        (log_in, doc_in, key_in, value_in, weight_in), (log, doc, key, value, weight), sems
    )
    copies[0].wait()
    copies[1].wait()
    _, down = running(log[...], doc[...], stage)
    final = down[BLOCK - 1 : BLOCK, :]
    kept = down[:, HEADS : HEADS + 1] == final[:, HEADS : HEADS + 1]
    to_end = jnp.where(kept, jnp.exp(final - down), 0.0)
    copies[2].wait()
    copies[3].wait()
    for h in range(HEADS):
        span = slice(h * HD, (h + 1) * HD)
        decayed = (key[:, span].astype(jnp.float32) * to_end[:, h : h + 1]).astype(jnp.bfloat16)
        state = dot(decayed, value[:, span], TN).astype(jnp.bfloat16)
        meta = meta_of(final[:, h : h + 1], final[:, HEADS : HEADS + 1])
        for half in range(2):
            out_ref[2 * h + half, 0:SLICE, :] = state[half * SLICE : (half + 1) * SLICE]
            out_ref[2 * h + half, SLICE:ROWS, :] = meta
    copies[4].wait()
    for k in range(RING):
        for j in range(4):
            out_ref[k, ROWS + 64 * j : ROWS + 64 * (j + 1), :] = weight[:, j * HD : (j + 1) * HD]


def row_kernel(states_ref, out_ref, weight_ref):
    total = jnp.zeros((SLICE, HD), jnp.float32)
    logs = jnp.zeros((1, HD), jnp.float32)
    prior = None
    for k in range(RING):
        log, last = read_meta(states_ref[k, SLICE:ROWS, :])
        if k:
            total = total * jnp.where(last == prior, jnp.exp(log), 0.0)
        total = total + states_ref[k, 0:SLICE, :].astype(jnp.float32)
        logs = logs + log
        prior = last
    for k in range(RING):
        out_ref[k, 0:SLICE, :] = total.astype(jnp.bfloat16)
        out_ref[k, SLICE:ROWS, :] = meta_of(logs, prior)
    weight_ref[...] = states_ref[:, ROWS:FULL, :]


def enter_kernel(states_ref, rows_ref, out_ref):
    here = lax.axis_index("y")
    entering = jnp.zeros((SLICE, HD), jnp.float32)
    memory = entering
    prior = jnp.zeros((1, HD), jnp.float32)
    prior_row = prior
    for k in range(RING):
        log, last = read_meta(rows_ref[k, SLICE:ROWS, :])
        memory = jnp.where(here == k, entering, memory)
        prior = jnp.where(here == k, prior_row, prior)
        entering = entering * jnp.where(last == prior_row, jnp.exp(log), 0.0)
        entering = entering + rows_ref[k, 0:SLICE, :].astype(jnp.float32)
        prior_row = last
    for k in range(RING):
        out_ref[k, 0:SLICE, :] = memory.astype(jnp.bfloat16)
        out_ref[k, SLICE:ROWS, :] = jnp.broadcast_to(prior, (16, HD)).astype(jnp.bfloat16)
        log, last = read_meta(states_ref[k, SLICE:ROWS, :])
        memory = memory * jnp.where(last == prior, jnp.exp(log), 0.0)
        memory = memory + states_ref[k, 0:SLICE, :].astype(jnp.float32)
        prior = last


def attend_kernel(
    log_in, doc_in, query_in, key_in, value_in, out_ref, down_ref,
    log, doc, query_ref, key_ref, value_ref, stage, mask, sems,
):
    copies = fetch(
        (log_in, doc_in, query_in, key_in, value_in), (log, doc, query_ref, key_ref, value_ref), sems
    )
    copies[0].wait()
    copies[1].wait()
    across, down = running(log[...], doc[...], stage)
    down_ref[...] = down
    doc_down = down[:, HEADS : HEADS + 1]
    row = lax.broadcasted_iota(jnp.int32, (BLOCK, BLOCK), 0)
    column = lax.broadcasted_iota(jnp.int32, (BLOCK, BLOCK), 1)
    seen = jnp.logical_and(row >= column, doc_down == across[HEADS : HEADS + 1, :])
    mask[...] = jnp.where(seen, 0.0, -1e30)
    part_rows = BLOCK // 2
    for copy in copies[2:]:
        copy.wait()
    for h in range(HEADS):
        span = slice(h * HD, (h + 1) * HD)
        for i in range(2):
            rows = slice(i * part_rows, (i + 1) * part_rows)
            seen = slice(0, (i + 1) * part_rows)
            scores = dot(query_ref[rows, span], key_ref[seen, span], NT)
            gap = down[rows, h : h + 1] - across[h : h + 1, seen] + mask[rows, seen]
            weighted = (scores * jnp.exp(gap)).astype(jnp.bfloat16)
            out_ref[rows, span] = dot(weighted, value_ref[seen, span])


def finish_kernel(
    down_in, memory_in, gain_in, query_in, local_in, out_ref,
    down_ref, memory_ref, gain_ref, query_ref, local_ref, sems,
):
    copies = fetch(
        (down_in, memory_in, gain_in, query_in, local_in),
        (down_ref, memory_ref, gain_ref, query_ref, local_ref),
        sems,
    )
    for copy in copies[:3]:
        copy.wait()
    down = down_ref[...]
    prior = memory_ref[0, SLICE : SLICE + 16, :].astype(jnp.float32)[0:1, 0:1]
    reach = jnp.where(down[:, HEADS : HEADS + 1] == prior, jnp.exp(down), 0.0)
    for copy in copies[3:]:
        copy.wait()
    for h in range(HEADS):
        span = slice(h * HD, (h + 1) * HD)
        memory = jnp.concatenate([memory_ref[2 * h, 0:SLICE, :], memory_ref[2 * h + 1, 0:SLICE, :]], axis=0)
        heads = local_ref[:, span] + reach[:, h : h + 1] * dot(query_ref[:, span], memory)
        scale = lax.rsqrt(jnp.mean(heads * heads, axis=-1, keepdims=True) + 1e-06)
        out_ref[:, span] = (heads * scale * gain_ref[:, span]).astype(jnp.bfloat16)


def unpack(held, s):
    return jnp.concatenate(
        [held[s, :, 64 * j : 64 * (j + 1), :].reshape(BLOCK, HD) for j in range(4)], axis=1
    )


def project_kernel(*refs):
    sources, (weight_in, out_ref, total, blocks, held, sems) = refs[:RING], refs[RING:]
    chips = lax.axis_size("x")
    x, c = lax.axis_index("x"), lax.axis_index("c")
    half = BLOCK // 2
    copies = []
    for s in range(RING):
        place = 2 * lax.rem(x + (0, -1, 1, 2)[s // 2] + chips, chips) + (1 - c if s % 2 else c)
        copies.append([pltpu.make_async_copy(weight_in.at[place], held.at[s], sems.at[s, 0])])
        copies[s].append(pltpu.make_async_copy(sources[s], blocks.at[s], sems.at[s, 1]))
        for copy in copies[s]:
            copy.start()
    for s in range(RING):
        for copy in copies[s]:
            copy.wait()
        for t in range(2):
            rows = slice(t * half, (t + 1) * half)
            product = dot(blocks[s, rows], unpack(held, s))
            if s == 0:
                total[rows] = product
            elif s < RING - 1:
                total[rows] += product
            else:
                out_ref[rows, :] = (total[rows] + product).astype(jnp.bfloat16)


def call(kernel, out_shape, args, specs, scratch=(), flops=0, transcendentals=0, grant=16):
    return pl.pallas_call(
        kernel,
        out_shape=out_shape,
        in_specs=specs,
        out_specs=jax.tree.map(lambda _: VMEM, out_shape),
        scratch_shapes=list(scratch),
        compiler_params=pltpu.CompilerParams(vmem_limit_bytes=grant * 2**20),
        cost_estimate=pl.CostEstimate(flops=flops, bytes_accessed=2**20, transcendentals=transcendentals),
    )(*args)


def local(sizes, queries, key_rows, value_rows, log_decay, doc_ids, head_gain, out_weight):
    nx = sizes[2]
    shape = lambda *dims: jax.ShapeDtypeStruct(dims, jnp.bfloat16)
    docs, gains = doc_ids.reshape(1, BLOCK), head_gain.reshape(1, -1)
    wide = pltpu.VMEM(queries.shape, jnp.bfloat16)
    logs_held = pltpu.VMEM(log_decay.shape, jnp.float32)
    docs_held = pltpu.VMEM(docs.shape, jnp.int32)
    stage = pltpu.VMEM((8, BLOCK), jnp.float32)

    states = call(
        state_kernel,
        shape(RING, FULL, HD),
        (log_decay, docs, key_rows, value_rows, out_weight),
        [ANY] * 5,
        [logs_held, docs_held, wide, wide, pltpu.VMEM(out_weight.shape, jnp.bfloat16), stage, pltpu.SemaphoreType.DMA((5,))],
        10**8,
        4096,
        GRANT,
    )
    states = lax.all_to_all(states, "z", 0, 0, tiled=True)
    rows, weight = call(
        row_kernel, (shape(RING, ROWS, HD), shape(RING, 256, HD)), (states,), [VMEM]
    )
    weight = lax.all_gather(weight, "y")
    rows = lax.all_to_all(rows, "y", 0, 0, tiled=True)
    entering = call(
        enter_kernel, shape(RING, ROWS, HD), (states, rows), [VMEM, VMEM]
    )
    entering = lax.all_to_all(entering, "z", 0, 0, tiled=True)

    alone, down = call(
        attend_kernel,
        (jax.ShapeDtypeStruct(queries.shape, jnp.float32), jax.ShapeDtypeStruct((BLOCK, 8), jnp.float32)),
        (log_decay, docs, queries, key_rows, value_rows),
        [ANY] * 5,
        [logs_held, docs_held, wide, wide, wide, stage, pltpu.VMEM((BLOCK, BLOCK), jnp.float32)]
        + [pltpu.SemaphoreType.DMA((5,))],
        6 * 10**8,
        2**20,
        GRANT,
    )
    normed = call(
        finish_kernel,
        shape(*queries.shape),
        (down, entering, gains, queries, alone),
        [ANY] * 5,
        [
            pltpu.VMEM(down.shape, jnp.float32),
            pltpu.VMEM(entering.shape, jnp.bfloat16),
            pltpu.VMEM(gains.shape, jnp.float32),
            wide,
            pltpu.VMEM(alone.shape, jnp.float32),
            pltpu.SemaphoreType.DMA((5,)),
        ],
        10**8,
        0,
        GRANT,
    )

    right = [(i, (i + 1) % nx) for i in range(nx)]
    left = [(i, (i - 1) % nx) for i in range(nx)]
    before = lax.ppermute(normed, "x", right)
    after = lax.ppermute(normed, "x", left)
    half = BLOCK // 2
    far_one = lax.ppermute(before[:half], "x", right)
    far_two = lax.ppermute(after[half:], "x", left)
    cross = lambda block: lax.ppermute(block, "c", [(0, 1), (1, 0)])

    near = [normed, cross(normed), before, cross(before), after, cross(after)]
    far = jnp.concatenate([far_one, far_two])
    far = [far, cross(far)]
    return call(
        project_kernel,
        shape(*queries.shape),
        (*near, *far, weight),
        [ANY] * 9,
        [
            pltpu.VMEM(queries.shape, jnp.float32),
            pltpu.VMEM((RING, *queries.shape), jnp.bfloat16),
            pltpu.VMEM(weight.shape, jnp.bfloat16),
            pltpu.SemaphoreType.DMA((RING, 2)),
        ],
        2 * 10**9,
        0,
        GRANT,
    )


def solution(mesh):
    sizes = (8, 8, 4, 2)
    split = Mesh(mesh.devices.reshape(sizes), ALL)
    ctx, tp = ("y", "z"), ("x", "c")
    return jax.shard_map(
        lambda *args: local(sizes, *args),
        mesh=split,
        in_specs=(P(ctx, tp), P(ctx, tp), P(ctx, tp), P(tp, ctx), P(ctx), P(tp), P(ctx, tp)),
        out_specs=P(ctx, tp),
        check_vma=False,
    )
```

```python
import jax
import jax.numpy as jnp
from jax import lax
from jax.experimental import pallas as pl
from jax.experimental.pallas import tpu as pltpu
from jax.sharding import Mesh, PartitionSpec as P

HD = 128
BLOCK = 512
HEADS = 4
RING = 8
SLICE = HEADS * HD // RING
ROWS = SLICE + 16
GRANT = 62
FULL = ROWS + 4 * 64
ALL = ("y", "z", "x", "c")
NT = (((1,), (1,)), ((), ()))
TN = (((0,), (0,)), ((), ()))
VMEM = pl.BlockSpec(memory_space=pltpu.VMEM)
ANY = pl.BlockSpec(memory_space=pl.ANY)
SMEM = pl.BlockSpec(memory_space=pltpu.SMEM)


def parts_of(value):
    high = value.astype(jnp.bfloat16)
    rest = value - high.astype(jnp.float32)
    middle = rest.astype(jnp.bfloat16)
    low = (rest - middle.astype(jnp.float32)).astype(jnp.bfloat16)
    return high, middle, low


def dot(a, b, dims=(((1,), (0,)), ((), ()))):
    return lax.dot_general(a, b, dims, preferred_element_type=jnp.float32)


def running(log, doc, stage):
    stage[...] = jnp.zeros_like(stage)
    stage[0:HEADS, :] = log
    total = stage[...]
    lane = lax.broadcasted_iota(jnp.int32, total.shape, 1)
    step = 1
    while step < BLOCK:
        total = total + jnp.where(lane >= step, pltpu.roll(total, step, 1), 0.0)
        step *= 2
    stage[0:HEADS, :] = total[0:HEADS, :]
    stage[HEADS : HEADS + 1, :] = doc.astype(jnp.float32)
    across = stage[...]
    return across, jnp.transpose(across)


def fetch(sources, targets, sems):
    copies = [pltpu.make_async_copy(s, t, sems.at[i]) for i, (s, t) in enumerate(zip(sources, targets))]
    for copy in copies:
        copy.start()
    return copies


def meta_of(log, last):
    row = lax.broadcasted_iota(jnp.int32, (16, HD), 0)
    high, middle, low = [part.astype(jnp.float32) for part in parts_of(log)]
    meta = jnp.where(row == 0, high, jnp.where(row == 1, middle, jnp.where(row == 2, low, 0.0)))
    return jnp.where(row == 3, last, meta).astype(jnp.bfloat16)


def read_meta(meta):
    meta = meta.astype(jnp.float32)
    return meta[0:1] + meta[1:2] + meta[2:3], meta[3:4]


def state_kernel(log_in, doc_in, key_in, value_in, weight_in, out_ref, log, doc, key, value, weight, stage, sems):
    copies = fetch(
        (log_in, doc_in, key_in, value_in, weight_in), (log, doc, key, value, weight), sems
    )
    copies[0].wait()
    copies[1].wait()
    _, down = running(log[...], doc[...], stage)
    final = down[BLOCK - 1 : BLOCK, :]
    kept = down[:, HEADS : HEADS + 1] == final[:, HEADS : HEADS + 1]
    to_end = jnp.where(kept, jnp.exp(final - down), 0.0)
    copies[2].wait()
    copies[3].wait()
    for h in range(HEADS):
        span = slice(h * HD, (h + 1) * HD)
        decayed = (key[:, span].astype(jnp.float32) * to_end[:, h : h + 1]).astype(jnp.bfloat16)
        state = dot(decayed, value[:, span], TN).astype(jnp.bfloat16)
        meta = meta_of(final[:, h : h + 1], final[:, HEADS : HEADS + 1])
        for half in range(2):
            out_ref[2 * h + half, 0:SLICE, :] = state[half * SLICE : (half + 1) * SLICE]
            out_ref[2 * h + half, SLICE:ROWS, :] = meta
    copies[4].wait()
    for k in range(RING):
        for j in range(4):
            out_ref[k, ROWS + 64 * j : ROWS + 64 * (j + 1), :] = weight[:, j * HD : (j + 1) * HD]


def row_kernel(states_ref, out_ref, weight_ref):
    total = jnp.zeros((SLICE, HD), jnp.float32)
    logs = jnp.zeros((1, HD), jnp.float32)
    prior = None
    for k in range(RING):
        log, last = read_meta(states_ref[k, SLICE:ROWS, :])
        if k:
            total = total * jnp.where(last == prior, jnp.exp(log), 0.0)
        total = total + states_ref[k, 0:SLICE, :].astype(jnp.float32)
        logs = logs + log
        prior = last
    for k in range(RING):
        out_ref[k, 0:SLICE, :] = total.astype(jnp.bfloat16)
        out_ref[k, SLICE:ROWS, :] = meta_of(logs, prior)
    weight_ref[...] = states_ref[:, ROWS:FULL, :]


def enter_kernel(states_ref, rows_ref, out_ref):
    here = lax.axis_index("y")
    entering = jnp.zeros((SLICE, HD), jnp.float32)
    memory = entering
    prior = jnp.zeros((1, HD), jnp.float32)
    prior_row = prior
    for k in range(RING):
        log, last = read_meta(rows_ref[k, SLICE:ROWS, :])
        memory = jnp.where(here == k, entering, memory)
        prior = jnp.where(here == k, prior_row, prior)
        entering = entering * jnp.where(last == prior_row, jnp.exp(log), 0.0)
        entering = entering + rows_ref[k, 0:SLICE, :].astype(jnp.float32)
        prior_row = last
    for k in range(RING):
        out_ref[k, 0:SLICE, :] = memory.astype(jnp.bfloat16)
        out_ref[k, SLICE:ROWS, :] = jnp.broadcast_to(prior, (16, HD)).astype(jnp.bfloat16)
        log, last = read_meta(states_ref[k, SLICE:ROWS, :])
        memory = memory * jnp.where(last == prior, jnp.exp(log), 0.0)
        memory = memory + states_ref[k, 0:SLICE, :].astype(jnp.float32)
        prior = last


def attend_kernel(
    log_in, doc_in, query_in, key_in, value_in, out_ref, across_ref,
    log, doc, query_ref, key_ref, value_ref, stage, mask, sems,
):
    copies = fetch(
        (log_in, doc_in, query_in, key_in, value_in), (log, doc, query_ref, key_ref, value_ref), sems
    )
    copies[0].wait()
    copies[1].wait()
    across, down = running(log[...], doc[...], stage)
    across_ref[...] = across
    doc_down = down[:, HEADS : HEADS + 1]
    row = lax.broadcasted_iota(jnp.int32, (BLOCK, BLOCK), 0)
    column = lax.broadcasted_iota(jnp.int32, (BLOCK, BLOCK), 1)
    seen = jnp.logical_and(row >= column, doc_down == across[HEADS : HEADS + 1, :])
    mask[...] = jnp.where(seen, 0.0, -1e30)
    part_rows = BLOCK // 2
    for copy in copies[2:]:
        copy.wait()
    for h in range(HEADS):
        span = slice(h * HD, (h + 1) * HD)
        for i in range(2):
            rows = slice(i * part_rows, (i + 1) * part_rows)
            seen = slice(0, (i + 1) * part_rows)
            scores = dot(query_ref[rows, span], key_ref[seen, span], NT)
            gap = down[rows, h : h + 1] - across[h : h + 1, seen] + mask[rows, seen]
            weighted = (scores * jnp.exp(gap)).astype(jnp.bfloat16)
            out_ref[rows, span] = dot(weighted, value_ref[seen, span]).astype(jnp.bfloat16)


def finish_kernel(
    across_in, memory_in, gain_in, query_in, local_in, out_ref,
    across_ref, memory_ref, gain_ref, query_ref, local_ref, sems,
):
    copies = fetch(
        (across_in, memory_in, gain_in, query_in, local_in),
        (across_ref, memory_ref, gain_ref, query_ref, local_ref),
        sems,
    )
    for copy in copies[:3]:
        copy.wait()
    across = across_ref[...]
    prior = memory_ref[0, SLICE : SLICE + 16, :].astype(jnp.float32)[0:1, 0:1]
    reach = jnp.transpose(jnp.where(across[HEADS : HEADS + 1, :] == prior, jnp.exp(across), 0.0))
    for copy in copies[3:]:
        copy.wait()
    for h in range(HEADS):
        span = slice(h * HD, (h + 1) * HD)
        memory = jnp.concatenate([memory_ref[2 * h, 0:SLICE, :], memory_ref[2 * h + 1, 0:SLICE, :]], axis=0)
        heads = local_ref[:, span].astype(jnp.float32) + reach[:, h : h + 1] * dot(query_ref[:, span], memory)
        scale = lax.rsqrt(jnp.mean(heads * heads, axis=-1, keepdims=True) + 1e-06)
        out_ref[:, span] = (heads * scale * gain_ref[:, span]).astype(jnp.bfloat16)


def unpack(held, s):
    return jnp.concatenate(
        [held[s, :, 64 * j : 64 * (j + 1), :].reshape(BLOCK, HD) for j in range(4)], axis=1
    )


def project_kernel(*refs):
    sources, (weight_in, out_ref, total, blocks, held, sems) = refs[:RING], refs[RING:]
    chips = lax.axis_size("x")
    x, c = lax.axis_index("x"), lax.axis_index("c")
    half = BLOCK // 2
    copies = []
    for s in range(RING):
        place = 2 * lax.rem(x + (0, -1, 1, 2)[s // 2] + chips, chips) + (1 - c if s % 2 else c)
        copies.append([pltpu.make_async_copy(weight_in.at[place], held.at[s], sems.at[s, 0])])
        copies[s].append(pltpu.make_async_copy(sources[s], blocks.at[s], sems.at[s, 1]))
        for copy in copies[s]:
            copy.start()
    for s in range(RING):
        for copy in copies[s]:
            copy.wait()
        for t in range(2):
            rows = slice(t * half, (t + 1) * half)
            product = dot(blocks[s, rows], unpack(held, s))
            if s == 0:
                total[rows] = product
            elif s < RING - 1:
                total[rows] += product
            else:
                out_ref[rows, :] = (total[rows] + product).astype(jnp.bfloat16)


def call(kernel, out_shape, args, specs, scratch=(), flops=0, transcendentals=0, grant=16):
    return pl.pallas_call(
        kernel,
        out_shape=out_shape,
        in_specs=specs,
        out_specs=jax.tree.map(lambda _: VMEM, out_shape),
        scratch_shapes=list(scratch),
        compiler_params=pltpu.CompilerParams(vmem_limit_bytes=grant * 2**20),
        cost_estimate=pl.CostEstimate(flops=flops, bytes_accessed=2**20, transcendentals=transcendentals),
    )(*args)


def local(sizes, queries, key_rows, value_rows, log_decay, doc_ids, head_gain, out_weight):
    nx = sizes[2]
    shape = lambda *dims: jax.ShapeDtypeStruct(dims, jnp.bfloat16)
    docs, gains = doc_ids.reshape(1, BLOCK), head_gain.reshape(1, -1)
    wide = pltpu.VMEM(queries.shape, jnp.bfloat16)
    logs_held = pltpu.VMEM(log_decay.shape, jnp.float32)
    docs_held = pltpu.VMEM(docs.shape, jnp.int32)
    stage = pltpu.VMEM((8, BLOCK), jnp.float32)

    states = call(
        state_kernel,
        shape(RING, FULL, HD),
        (log_decay, docs, key_rows, value_rows, out_weight),
        [ANY] * 5,
        [logs_held, docs_held, wide, wide, pltpu.VMEM(out_weight.shape, jnp.bfloat16), stage, pltpu.SemaphoreType.DMA((5,))],
        10**8,
        4096,
        GRANT,
    )
    states = lax.all_to_all(states, "z", 0, 0, tiled=True)
    rows, weight = call(
        row_kernel, (shape(RING, ROWS, HD), shape(RING, 256, HD)), (states,), [VMEM]
    )
    weight = lax.all_gather(weight, "y")
    rows = lax.all_to_all(rows, "y", 0, 0, tiled=True)
    entering = call(
        enter_kernel, shape(RING, ROWS, HD), (states, rows), [VMEM, VMEM]
    )
    entering = lax.all_to_all(entering, "z", 0, 0, tiled=True)

    alone, across = call(
        attend_kernel,
        (shape(*queries.shape), jax.ShapeDtypeStruct((8, BLOCK), jnp.float32)),
        (log_decay, docs, queries, key_rows, value_rows),
        [ANY] * 5,
        [logs_held, docs_held, wide, wide, wide, stage, pltpu.VMEM((BLOCK, BLOCK), jnp.float32)]
        + [pltpu.SemaphoreType.DMA((5,))],
        6 * 10**8,
        2**20,
        GRANT,
    )
    normed = call(
        finish_kernel,
        shape(*queries.shape),
        (across, entering, gains, queries, alone),
        [ANY] * 5,
        [
            pltpu.VMEM(across.shape, jnp.float32),
            pltpu.VMEM(entering.shape, jnp.bfloat16),
            pltpu.VMEM(gains.shape, jnp.float32),
            wide,
            wide,
            pltpu.SemaphoreType.DMA((5,)),
        ],
        10**8,
        0,
        32,
    )

    right = [(i, (i + 1) % nx) for i in range(nx)]
    left = [(i, (i - 1) % nx) for i in range(nx)]
    before = lax.ppermute(normed, "x", right)
    after = lax.ppermute(normed, "x", left)
    far = lax.ppermute(before, "x", right)
    cross = lambda block: lax.ppermute(block, "c", [(0, 1), (1, 0)])

    near = [normed, cross(normed), before, cross(before), after, cross(after)]
    far = [far, cross(far)]
    return call(
        project_kernel,
        shape(*queries.shape),
        (*near, *far, weight),
        [ANY] * 9,
        [
            pltpu.VMEM(queries.shape, jnp.float32),
            pltpu.VMEM((RING, *queries.shape), jnp.bfloat16),
            pltpu.VMEM(weight.shape, jnp.bfloat16),
            pltpu.SemaphoreType.DMA((RING, 2)),
        ],
        2 * 10**9,
        0,
        GRANT,
    )


def solution(mesh):
    sizes = (8, 8, 4, 2)
    split = Mesh(mesh.devices.reshape(sizes), ALL)
    ctx, tp = ("y", "z"), ("x", "c")
    return jax.shard_map(
        lambda *args: local(sizes, *args),
        mesh=split,
        in_specs=(P(ctx, tp), P(ctx, tp), P(ctx, tp), P(tp, ctx), P(ctx), P(tp), P(ctx, tp)),
        out_specs=P(ctx, tp),
        check_vma=False,
    )
```

```python
import jax
import jax.numpy as jnp
from jax import lax
from jax.experimental import pallas as pl
from jax.experimental.pallas import tpu as pltpu
from jax.sharding import Mesh, PartitionSpec as P

HD = 128
BLOCK = 512
HEADS = 4
RING = 8
SLICE = HEADS * HD // RING
ROWS = SLICE + 16
GRANT = 62
FULL = ROWS + 4 * 64
ALL = ("y", "z", "x", "c")
NT = (((1,), (1,)), ((), ()))
TN = (((0,), (0,)), ((), ()))
VMEM = pl.BlockSpec(memory_space=pltpu.VMEM)
ANY = pl.BlockSpec(memory_space=pl.ANY)
SMEM = pl.BlockSpec(memory_space=pltpu.SMEM)


def parts_of(value):
    high = value.astype(jnp.bfloat16)
    rest = value - high.astype(jnp.float32)
    middle = rest.astype(jnp.bfloat16)
    low = (rest - middle.astype(jnp.float32)).astype(jnp.bfloat16)
    return high, middle, low


def dot(a, b, dims=(((1,), (0,)), ((), ()))):
    return lax.dot_general(a, b, dims, preferred_element_type=jnp.float32)


def running(log, doc, stage):
    stage[...] = jnp.zeros_like(stage)
    stage[0:HEADS, :] = log
    total = stage[...]
    lane = lax.broadcasted_iota(jnp.int32, total.shape, 1)
    step = 1
    while step < BLOCK:
        total = total + jnp.where(lane >= step, pltpu.roll(total, step, 1), 0.0)
        step *= 2
    stage[0:HEADS, :] = total[0:HEADS, :]
    stage[HEADS : HEADS + 1, :] = doc.astype(jnp.float32)
    across = stage[...]
    return across, jnp.transpose(across)


def fetch(sources, targets, sems):
    copies = [pltpu.make_async_copy(s, t, sems.at[i]) for i, (s, t) in enumerate(zip(sources, targets))]
    for copy in copies:
        copy.start()
    return copies


def meta_of(log, last):
    row = lax.broadcasted_iota(jnp.int32, (16, HD), 0)
    high, middle, low = [part.astype(jnp.float32) for part in parts_of(log)]
    meta = jnp.where(row == 0, high, jnp.where(row == 1, middle, jnp.where(row == 2, low, 0.0)))
    return jnp.where(row == 3, last, meta).astype(jnp.bfloat16)


def read_meta(meta):
    meta = meta.astype(jnp.float32)
    return meta[0:1] + meta[1:2] + meta[2:3], meta[3:4]


def state_kernel(log_in, doc_in, key_in, value_in, weight_in, out_ref, log, doc, key, value, weight, stage, sems):
    copies = fetch(
        (log_in, doc_in, key_in, value_in, weight_in), (log, doc, key, value, weight), sems
    )
    copies[0].wait()
    copies[1].wait()
    _, down = running(log[...], doc[...], stage)
    final = down[BLOCK - 1 : BLOCK, :]
    kept = down[:, HEADS : HEADS + 1] == final[:, HEADS : HEADS + 1]
    to_end = jnp.where(kept, jnp.exp(final - down), 0.0)
    copies[2].wait()
    copies[3].wait()
    for h in range(HEADS):
        span = slice(h * HD, (h + 1) * HD)
        decayed = (key[:, span].astype(jnp.float32) * to_end[:, h : h + 1]).astype(jnp.bfloat16)
        state = dot(decayed, value[:, span], TN).astype(jnp.bfloat16)
        meta = meta_of(final[:, h : h + 1], final[:, HEADS : HEADS + 1])
        for half in range(2):
            out_ref[2 * h + half, 0:SLICE, :] = state[half * SLICE : (half + 1) * SLICE]
            out_ref[2 * h + half, SLICE:ROWS, :] = meta
    copies[4].wait()
    for k in range(RING):
        for j in range(4):
            out_ref[k, ROWS + 64 * j : ROWS + 64 * (j + 1), :] = weight[:, j * HD : (j + 1) * HD]


def row_kernel(states_ref, out_ref, weight_ref):
    total = jnp.zeros((SLICE, HD), jnp.float32)
    logs = jnp.zeros((1, HD), jnp.float32)
    prior = None
    for k in range(RING):
        log, last = read_meta(states_ref[k, SLICE:ROWS, :])
        if k:
            total = total * jnp.where(last == prior, jnp.exp(log), 0.0)
        total = total + states_ref[k, 0:SLICE, :].astype(jnp.float32)
        logs = logs + log
        prior = last
    for k in range(RING):
        out_ref[k, 0:SLICE, :] = total.astype(jnp.bfloat16)
        out_ref[k, SLICE:ROWS, :] = meta_of(logs, prior)
    weight_ref[...] = states_ref[:, ROWS:FULL, :]


def enter_kernel(states_ref, rows_ref, out_ref):
    here = lax.axis_index("y")
    entering = jnp.zeros((SLICE, HD), jnp.float32)
    memory = entering
    prior = jnp.zeros((1, HD), jnp.float32)
    prior_row = prior
    for k in range(RING):
        log, last = read_meta(rows_ref[k, SLICE:ROWS, :])
        memory = jnp.where(here == k, entering, memory)
        prior = jnp.where(here == k, prior_row, prior)
        entering = entering * jnp.where(last == prior_row, jnp.exp(log), 0.0)
        entering = entering + rows_ref[k, 0:SLICE, :].astype(jnp.float32)
        prior_row = last
    for k in range(RING):
        out_ref[k, 0:SLICE, :] = memory.astype(jnp.bfloat16)
        out_ref[k, SLICE:ROWS, :] = jnp.broadcast_to(prior, (16, HD)).astype(jnp.bfloat16)
        log, last = read_meta(states_ref[k, SLICE:ROWS, :])
        memory = memory * jnp.where(last == prior, jnp.exp(log), 0.0)
        memory = memory + states_ref[k, 0:SLICE, :].astype(jnp.float32)
        prior = last


def attend_kernel(
    log_in, doc_in, query_in, key_in, value_in, out_ref, across_ref,
    log, doc, query_ref, key_ref, value_ref, stage, mask, sems,
):
    copies = fetch(
        (log_in, doc_in, query_in, key_in, value_in), (log, doc, query_ref, key_ref, value_ref), sems
    )
    copies[0].wait()
    copies[1].wait()
    across, down = running(log[...], doc[...], stage)
    across_ref[...] = across
    doc_down = down[:, HEADS : HEADS + 1]
    row = lax.broadcasted_iota(jnp.int32, (BLOCK, BLOCK), 0)
    column = lax.broadcasted_iota(jnp.int32, (BLOCK, BLOCK), 1)
    seen = jnp.logical_and(row >= column, doc_down == across[HEADS : HEADS + 1, :])
    mask[...] = jnp.where(seen, 0.0, -1e30)
    part_rows = BLOCK // 2
    for copy in copies[2:]:
        copy.wait()
    for h in range(HEADS):
        span = slice(h * HD, (h + 1) * HD)
        for i in range(2):
            rows = slice(i * part_rows, (i + 1) * part_rows)
            seen = slice(0, (i + 1) * part_rows)
            scores = dot(query_ref[rows, span], key_ref[seen, span], NT)
            gap = down[rows, h : h + 1] - across[h : h + 1, seen] + mask[rows, seen]
            weighted = (scores * jnp.exp(gap)).astype(jnp.bfloat16)
            out_ref[rows, span] = dot(weighted, value_ref[seen, span]).astype(jnp.bfloat16)


def finish_kernel(
    across_in, memory_in, gain_in, query_in, local_in, out_ref,
    across_ref, memory_ref, gain_ref, query_ref, local_ref, sems,
):
    copies = fetch(
        (across_in, memory_in, gain_in, query_in, local_in),
        (across_ref, memory_ref, gain_ref, query_ref, local_ref),
        sems,
    )
    for copy in copies[:3]:
        copy.wait()
    across = across_ref[...]
    prior = memory_ref[0, SLICE : SLICE + 16, :].astype(jnp.float32)[0:1, 0:1]
    reach = jnp.transpose(jnp.where(across[HEADS : HEADS + 1, :] == prior, jnp.exp(across), 0.0))
    for copy in copies[3:]:
        copy.wait()
    for h in range(HEADS):
        span = slice(h * HD, (h + 1) * HD)
        memory = jnp.concatenate([memory_ref[2 * h, 0:SLICE, :], memory_ref[2 * h + 1, 0:SLICE, :]], axis=0)
        heads = local_ref[:, span].astype(jnp.float32) + reach[:, h : h + 1] * dot(query_ref[:, span], memory)
        scale = lax.rsqrt(jnp.mean(heads * heads, axis=-1, keepdims=True) + 1e-06)
        out_ref[:, span] = (heads * scale * gain_ref[:, span]).astype(jnp.bfloat16)


def unpack(held, s):
    return jnp.concatenate(
        [held[s, :, 64 * j : 64 * (j + 1), :].reshape(BLOCK, HD) for j in range(4)], axis=1
    )


def project_kernel(*refs):
    sources, (weight_in, out_ref, total, blocks, held, sems) = refs[:RING], refs[RING:]
    chips = lax.axis_size("x")
    x, c = lax.axis_index("x"), lax.axis_index("c")
    half = BLOCK // 2
    copies = []
    for s in range(RING):
        place = 2 * lax.rem(x + (0, -1, 1, 2)[s // 2] + chips, chips) + (1 - c if s % 2 else c)
        copies.append([pltpu.make_async_copy(weight_in.at[place], held.at[s], sems.at[s, 0])])
        copies[s].append(pltpu.make_async_copy(sources[s], blocks.at[s], sems.at[s, 1]))
        for copy in copies[s]:
            copy.start()
    for s in range(RING):
        for copy in copies[s]:
            copy.wait()
        for t in range(2):
            rows = slice(t * half, (t + 1) * half)
            product = dot(blocks[s, rows], unpack(held, s))
            if s == 0:
                total[rows] = product
            elif s < RING - 1:
                total[rows] += product
            else:
                out_ref[rows, :] = (total[rows] + product).astype(jnp.bfloat16)


def call(kernel, out_shape, args, specs, scratch=(), flops=0, transcendentals=0, grant=16):
    return pl.pallas_call(
        kernel,
        out_shape=out_shape,
        in_specs=specs,
        out_specs=jax.tree.map(lambda _: VMEM, out_shape),
        scratch_shapes=list(scratch),
        compiler_params=pltpu.CompilerParams(vmem_limit_bytes=grant * 2**20),
        cost_estimate=pl.CostEstimate(flops=flops, bytes_accessed=2**20, transcendentals=transcendentals),
    )(*args)


def local(sizes, queries, key_rows, value_rows, log_decay, doc_ids, head_gain, out_weight):
    nx = sizes[2]
    shape = lambda *dims: jax.ShapeDtypeStruct(dims, jnp.bfloat16)
    docs, gains = doc_ids.reshape(1, BLOCK), head_gain.reshape(1, -1)
    wide = pltpu.VMEM(queries.shape, jnp.bfloat16)
    logs_held = pltpu.VMEM(log_decay.shape, jnp.float32)
    docs_held = pltpu.VMEM(docs.shape, jnp.int32)
    stage = pltpu.VMEM((8, BLOCK), jnp.float32)

    states = call(
        state_kernel,
        shape(RING, FULL, HD),
        (log_decay, docs, key_rows, value_rows, out_weight),
        [ANY] * 5,
        [logs_held, docs_held, wide, wide, pltpu.VMEM(out_weight.shape, jnp.bfloat16), stage, pltpu.SemaphoreType.DMA((5,))],
        10**8,
        4096,
        GRANT,
    )
    states = lax.all_to_all(states, "z", 0, 0, tiled=True)
    rows, weight = call(
        row_kernel, (shape(RING, ROWS, HD), shape(RING, 256, HD)), (states,), [VMEM]
    )
    weight = lax.all_gather(weight, "y")
    rows = lax.all_to_all(rows, "y", 0, 0, tiled=True)
    entering = call(
        enter_kernel, shape(RING, ROWS, HD), (states, rows), [VMEM, VMEM]
    )
    entering = lax.all_to_all(entering, "z", 0, 0, tiled=True)

    alone, across = call(
        attend_kernel,
        (shape(*queries.shape), jax.ShapeDtypeStruct((8, BLOCK), jnp.float32)),
        (log_decay, docs, queries, key_rows, value_rows),
        [ANY] * 5,
        [logs_held, docs_held, wide, wide, wide, stage, pltpu.VMEM((BLOCK, BLOCK), jnp.float32)]
        + [pltpu.SemaphoreType.DMA((5,))],
        6 * 10**8,
        2**20,
        32,
    )
    normed = call(
        finish_kernel,
        shape(*queries.shape),
        (across, entering, gains, queries, alone),
        [ANY] * 5,
        [
            pltpu.VMEM(across.shape, jnp.float32),
            pltpu.VMEM(entering.shape, jnp.bfloat16),
            pltpu.VMEM(gains.shape, jnp.float32),
            wide,
            wide,
            pltpu.SemaphoreType.DMA((5,)),
        ],
        10**8,
        0,
        32,
    )

    right = [(i, (i + 1) % nx) for i in range(nx)]
    left = [(i, (i - 1) % nx) for i in range(nx)]
    before = lax.ppermute(normed, "x", right)
    after = lax.ppermute(normed, "x", left)
    far = lax.ppermute(before, "x", right)
    cross = lambda block: lax.ppermute(block, "c", [(0, 1), (1, 0)])

    near = [normed, cross(normed), before, cross(before), after, cross(after)]
    far = [far, cross(far)]
    return call(
        project_kernel,
        shape(*queries.shape),
        (*near, *far, weight),
        [ANY] * 9,
        [
            pltpu.VMEM(queries.shape, jnp.float32),
            pltpu.VMEM((RING, *queries.shape), jnp.bfloat16),
            pltpu.VMEM(weight.shape, jnp.bfloat16),
            pltpu.SemaphoreType.DMA((RING, 2)),
        ],
        2 * 10**9,
        0,
        58,
    )


def solution(mesh):
    sizes = (8, 8, 4, 2)
    split = Mesh(mesh.devices.reshape(sizes), ALL)
    ctx, tp = ("y", "z"), ("x", "c")
    return jax.shard_map(
        lambda *args: local(sizes, *args),
        mesh=split,
        in_specs=(P(ctx, tp), P(ctx, tp), P(ctx, tp), P(tp, ctx), P(ctx), P(tp), P(ctx, tp)),
        out_specs=P(ctx, tp),
        check_vma=False,
    )
```

```python
import jax
import jax.numpy as jnp
from jax import lax
from jax.experimental import pallas as pl
from jax.experimental.pallas import tpu as pltpu
from jax.sharding import Mesh, PartitionSpec as P

HD = 128
BLOCK = 512
HEADS = 4
RING = 8
SLICE = HEADS * HD // RING
ROWS = SLICE + 16
GRANT = 62
FULL = ROWS + 4 * 64
ALL = ("y", "z", "x", "c")
NT = (((1,), (1,)), ((), ()))
TN = (((0,), (0,)), ((), ()))
VMEM = pl.BlockSpec(memory_space=pltpu.VMEM)
ANY = pl.BlockSpec(memory_space=pl.ANY)
SMEM = pl.BlockSpec(memory_space=pltpu.SMEM)


def parts_of(value):
    high = value.astype(jnp.bfloat16)
    rest = value - high.astype(jnp.float32)
    middle = rest.astype(jnp.bfloat16)
    low = (rest - middle.astype(jnp.float32)).astype(jnp.bfloat16)
    return high, middle, low


def dot(a, b, dims=(((1,), (0,)), ((), ()))):
    return lax.dot_general(a, b, dims, preferred_element_type=jnp.float32)


def running(log, doc, stage):
    stage[...] = jnp.zeros_like(stage)
    stage[0:HEADS, :] = log
    total = stage[...]
    lane = lax.broadcasted_iota(jnp.int32, total.shape, 1)
    step = 1
    while step < BLOCK:
        total = total + jnp.where(lane >= step, pltpu.roll(total, step, 1), 0.0)
        step *= 2
    stage[0:HEADS, :] = total[0:HEADS, :]
    stage[HEADS : HEADS + 1, :] = doc.astype(jnp.float32)
    across = stage[...]
    return across, jnp.transpose(across)


def fetch(sources, targets, sems):
    copies = [pltpu.make_async_copy(s, t, sems.at[i]) for i, (s, t) in enumerate(zip(sources, targets))]
    for copy in copies:
        copy.start()
    return copies


def meta_of(log, last):
    row = lax.broadcasted_iota(jnp.int32, (16, HD), 0)
    high, middle, low = [part.astype(jnp.float32) for part in parts_of(log)]
    meta = jnp.where(row == 0, high, jnp.where(row == 1, middle, jnp.where(row == 2, low, 0.0)))
    return jnp.where(row == 3, last, meta).astype(jnp.bfloat16)


def read_meta(meta):
    meta = meta.astype(jnp.float32)
    return meta[0:1] + meta[1:2] + meta[2:3], meta[3:4]


def state_kernel(log_in, doc_in, key_in, value_in, weight_in, out_ref, log, doc, key, value, weight, stage, sems):
    copies = fetch(
        (log_in, doc_in, key_in, value_in, weight_in), (log, doc, key, value, weight), sems
    )
    copies[0].wait()
    copies[1].wait()
    _, down = running(log[...], doc[...], stage)
    final = down[BLOCK - 1 : BLOCK, :]
    kept = down[:, HEADS : HEADS + 1] == final[:, HEADS : HEADS + 1]
    to_end = jnp.where(kept, jnp.exp(final - down), 0.0)
    copies[2].wait()
    copies[3].wait()
    for h in range(HEADS):
        span = slice(h * HD, (h + 1) * HD)
        decayed = (key[:, span].astype(jnp.float32) * to_end[:, h : h + 1]).astype(jnp.bfloat16)
        state = dot(decayed, value[:, span], TN).astype(jnp.bfloat16)
        meta = meta_of(final[:, h : h + 1], final[:, HEADS : HEADS + 1])
        for half in range(2):
            out_ref[2 * h + half, 0:SLICE, :] = state[half * SLICE : (half + 1) * SLICE]
            out_ref[2 * h + half, SLICE:ROWS, :] = meta
    copies[4].wait()
    for k in range(RING):
        for j in range(4):
            out_ref[k, ROWS + 64 * j : ROWS + 64 * (j + 1), :] = weight[:, j * HD : (j + 1) * HD]


def row_kernel(states_ref, out_ref, weight_ref):
    total = jnp.zeros((SLICE, HD), jnp.float32)
    logs = jnp.zeros((1, HD), jnp.float32)
    prior = None
    for k in range(RING):
        log, last = read_meta(states_ref[k, SLICE:ROWS, :])
        if k:
            total = total * jnp.where(last == prior, jnp.exp(log), 0.0)
        total = total + states_ref[k, 0:SLICE, :].astype(jnp.float32)
        logs = logs + log
        prior = last
    for k in range(RING):
        out_ref[k, 0:SLICE, :] = total.astype(jnp.bfloat16)
        out_ref[k, SLICE:ROWS, :] = meta_of(logs, prior)
    weight_ref[...] = states_ref[:, ROWS:FULL, :]


def enter_kernel(states_ref, rows_ref, out_ref):
    here = lax.axis_index("y")
    entering = jnp.zeros((SLICE, HD), jnp.float32)
    memory = entering
    prior = jnp.zeros((1, HD), jnp.float32)
    prior_row = prior
    for k in range(RING):
        log, last = read_meta(rows_ref[k, SLICE:ROWS, :])
        memory = jnp.where(here == k, entering, memory)
        prior = jnp.where(here == k, prior_row, prior)
        entering = entering * jnp.where(last == prior_row, jnp.exp(log), 0.0)
        entering = entering + rows_ref[k, 0:SLICE, :].astype(jnp.float32)
        prior_row = last
    for k in range(RING):
        out_ref[k, 0:SLICE, :] = memory.astype(jnp.bfloat16)
        out_ref[k, SLICE:ROWS, :] = jnp.broadcast_to(prior, (16, HD)).astype(jnp.bfloat16)
        log, last = read_meta(states_ref[k, SLICE:ROWS, :])
        memory = memory * jnp.where(last == prior, jnp.exp(log), 0.0)
        memory = memory + states_ref[k, 0:SLICE, :].astype(jnp.float32)
        prior = last


def attend_kernel(
    log_in, doc_in, query_in, key_in, value_in, out_ref, across_ref,
    log, doc, query_ref, key_ref, value_ref, stage, mask, sems,
):
    copies = fetch(
        (log_in, doc_in, query_in, key_in, value_in), (log, doc, query_ref, key_ref, value_ref), sems
    )
    copies[0].wait()
    copies[1].wait()
    across, down = running(log[...], doc[...], stage)
    across_ref[...] = across
    doc_down = down[:, HEADS : HEADS + 1]
    row = lax.broadcasted_iota(jnp.int32, (BLOCK, BLOCK), 0)
    column = lax.broadcasted_iota(jnp.int32, (BLOCK, BLOCK), 1)
    seen = jnp.logical_and(row >= column, doc_down == across[HEADS : HEADS + 1, :])
    mask[...] = jnp.where(seen, 0.0, -1e30)
    part_rows = BLOCK // 2
    for copy in copies[2:]:
        copy.wait()
    for h in range(HEADS):
        span = slice(h * HD, (h + 1) * HD)
        for i in range(2):
            rows = slice(i * part_rows, (i + 1) * part_rows)
            seen = slice(0, (i + 1) * part_rows)
            scores = dot(query_ref[rows, span], key_ref[seen, span], NT)
            gap = down[rows, h : h + 1] - across[h : h + 1, seen] + mask[rows, seen]
            weighted = (scores * jnp.exp(gap)).astype(jnp.bfloat16)
            out_ref[rows, span] = dot(weighted, value_ref[seen, span]).astype(jnp.bfloat16)


def finish_kernel(
    across_in, memory_in, gain_in, query_in, local_in, out_ref,
    across_ref, memory_ref, gain_ref, query_ref, local_ref, sems,
):
    copies = fetch(
        (across_in, memory_in, gain_in, query_in, local_in),
        (across_ref, memory_ref, gain_ref, query_ref, local_ref),
        sems,
    )
    for copy in copies[:3]:
        copy.wait()
    across = across_ref[...]
    prior = memory_ref[0, SLICE : SLICE + 16, :].astype(jnp.float32)[0:1, 0:1]
    reach = jnp.transpose(jnp.where(across[HEADS : HEADS + 1, :] == prior, jnp.exp(across), 0.0))
    for copy in copies[3:]:
        copy.wait()
    for h in range(HEADS):
        span = slice(h * HD, (h + 1) * HD)
        memory = jnp.concatenate([memory_ref[2 * h, 0:SLICE, :], memory_ref[2 * h + 1, 0:SLICE, :]], axis=0)
        heads = local_ref[:, span].astype(jnp.float32) + reach[:, h : h + 1] * dot(query_ref[:, span], memory)
        scale = lax.rsqrt(jnp.mean(heads * heads, axis=-1, keepdims=True) + 1e-06)
        out_ref[:, span] = (heads * scale * gain_ref[:, span]).astype(jnp.bfloat16)


def unpack(held, s):
    return jnp.concatenate(
        [held[s, :, 64 * j : 64 * (j + 1), :].reshape(BLOCK, HD) for j in range(4)], axis=1
    )


def half_kernel(block_ref, crossed_ref, out_ref):
    del crossed_ref
    out_ref[...] = block_ref[out_ref.shape[0] :, :]


def project_kernel(*refs):
    sources, (weight_in, out_ref, total, blocks, held, sems) = refs[:RING], refs[RING:]
    chips = lax.axis_size("x")
    x, c = lax.axis_index("x"), lax.axis_index("c")
    half = BLOCK // 2
    copies = []
    for s in range(RING):
        place = 2 * lax.rem(x + (0, -1, 1, 2)[s // 2] + chips, chips) + (1 - c if s % 2 else c)
        copies.append([pltpu.make_async_copy(weight_in.at[place], held.at[s], sems.at[s, 0])])
        copies[s].append(pltpu.make_async_copy(sources[s], blocks.at[s], sems.at[s, 1]))
        for copy in copies[s]:
            copy.start()
    for s in range(RING):
        for copy in copies[s]:
            copy.wait()
        for t in range(2):
            rows = slice(t * half, (t + 1) * half)
            product = dot(blocks[s, rows], unpack(held, s))
            if s == 0:
                total[rows] = product
            elif s < RING - 1:
                total[rows] += product
            else:
                out_ref[rows, :] = (total[rows] + product).astype(jnp.bfloat16)


def call(kernel, out_shape, args, specs, scratch=(), flops=0, transcendentals=0, grant=16):
    return pl.pallas_call(
        kernel,
        out_shape=out_shape,
        in_specs=specs,
        out_specs=jax.tree.map(lambda _: VMEM, out_shape),
        scratch_shapes=list(scratch),
        compiler_params=pltpu.CompilerParams(vmem_limit_bytes=grant * 2**20),
        cost_estimate=pl.CostEstimate(flops=flops, bytes_accessed=2**20, transcendentals=transcendentals),
    )(*args)


def local(sizes, queries, key_rows, value_rows, log_decay, doc_ids, head_gain, out_weight):
    nx = sizes[2]
    shape = lambda *dims: jax.ShapeDtypeStruct(dims, jnp.bfloat16)
    docs, gains = doc_ids.reshape(1, BLOCK), head_gain.reshape(1, -1)
    wide = pltpu.VMEM(queries.shape, jnp.bfloat16)
    logs_held = pltpu.VMEM(log_decay.shape, jnp.float32)
    docs_held = pltpu.VMEM(docs.shape, jnp.int32)
    stage = pltpu.VMEM((8, BLOCK), jnp.float32)

    states = call(
        state_kernel,
        shape(RING, FULL, HD),
        (log_decay, docs, key_rows, value_rows, out_weight),
        [ANY] * 5,
        [logs_held, docs_held, wide, wide, pltpu.VMEM(out_weight.shape, jnp.bfloat16), stage, pltpu.SemaphoreType.DMA((5,))],
        10**8,
        4096,
        GRANT,
    )
    states = lax.all_to_all(states, "z", 0, 0, tiled=True)
    rows, weight = call(
        row_kernel, (shape(RING, ROWS, HD), shape(RING, 256, HD)), (states,), [VMEM]
    )
    weight = lax.all_gather(weight, "y")
    rows = lax.all_to_all(rows, "y", 0, 0, tiled=True)
    entering = call(
        enter_kernel, shape(RING, ROWS, HD), (states, rows), [VMEM, VMEM]
    )
    entering = lax.all_to_all(entering, "z", 0, 0, tiled=True)

    alone, across = call(
        attend_kernel,
        (shape(*queries.shape), jax.ShapeDtypeStruct((8, BLOCK), jnp.float32)),
        (log_decay, docs, queries, key_rows, value_rows),
        [ANY] * 5,
        [logs_held, docs_held, wide, wide, wide, stage, pltpu.VMEM((BLOCK, BLOCK), jnp.float32)]
        + [pltpu.SemaphoreType.DMA((5,))],
        6 * 10**8,
        2**20,
        32,
    )
    normed = call(
        finish_kernel,
        shape(*queries.shape),
        (across, entering, gains, queries, alone),
        [ANY] * 5,
        [
            pltpu.VMEM(across.shape, jnp.float32),
            pltpu.VMEM(entering.shape, jnp.bfloat16),
            pltpu.VMEM(gains.shape, jnp.float32),
            wide,
            wide,
            pltpu.SemaphoreType.DMA((5,)),
        ],
        10**8,
        0,
        32,
    )

    right = [(i, (i + 1) % nx) for i in range(nx)]
    left = [(i, (i - 1) % nx) for i in range(nx)]
    before = lax.ppermute(normed, "x", right)
    after = lax.ppermute(normed, "x", left)
    half = BLOCK // 2
    crossed = lax.ppermute(normed, "c", [(0, 1), (1, 0)])
    last = call(half_kernel, shape(half, queries.shape[1]), (after, crossed), [VMEM, ANY])
    far_one = lax.ppermute(before[:half], "x", right)
    far_two = lax.ppermute(last, "x", left)
    cross = lambda block: lax.ppermute(block, "c", [(0, 1), (1, 0)])

    near = [normed, crossed, before, cross(before), after, cross(after)]
    far = jnp.concatenate([far_one, far_two])
    far = [far, cross(far)]
    return call(
        project_kernel,
        shape(*queries.shape),
        (*near, *far, weight),
        [ANY] * 9,
        [
            pltpu.VMEM(queries.shape, jnp.float32),
            pltpu.VMEM((RING, *queries.shape), jnp.bfloat16),
            pltpu.VMEM(weight.shape, jnp.bfloat16),
            pltpu.SemaphoreType.DMA((RING, 2)),
        ],
        2 * 10**9,
        0,
        58,
    )


def solution(mesh):
    sizes = (8, 8, 4, 2)
    split = Mesh(mesh.devices.reshape(sizes), ALL)
    ctx, tp = ("y", "z"), ("x", "c")
    return jax.shard_map(
        lambda *args: local(sizes, *args),
        mesh=split,
        in_specs=(P(ctx, tp), P(ctx, tp), P(ctx, tp), P(tp, ctx), P(ctx), P(tp), P(ctx, tp)),
        out_specs=P(ctx, tp),
        check_vma=False,
    )
```

```python
import jax
import jax.numpy as jnp
from jax import lax
from jax.experimental import pallas as pl
from jax.experimental.pallas import tpu as pltpu
from jax.sharding import Mesh, PartitionSpec as P

HD = 128
BLOCK = 512
HEADS = 4
RING = 8
SLICE = HEADS * HD // RING
ROWS = SLICE + 16
GRANT = 62
FULL = ROWS + 4 * 64
ALL = ("y", "z", "x", "c")
NT = (((1,), (1,)), ((), ()))
TN = (((0,), (0,)), ((), ()))
VMEM = pl.BlockSpec(memory_space=pltpu.VMEM)
ANY = pl.BlockSpec(memory_space=pl.ANY)
SMEM = pl.BlockSpec(memory_space=pltpu.SMEM)


def parts_of(value):
    high = value.astype(jnp.bfloat16)
    rest = value - high.astype(jnp.float32)
    middle = rest.astype(jnp.bfloat16)
    low = (rest - middle.astype(jnp.float32)).astype(jnp.bfloat16)
    return high, middle, low


def dot(a, b, dims=(((1,), (0,)), ((), ()))):
    return lax.dot_general(a, b, dims, preferred_element_type=jnp.float32)


def running(log, doc, stage):
    stage[...] = jnp.zeros_like(stage)
    stage[0:HEADS, :] = log
    total = stage[...]
    lane = lax.broadcasted_iota(jnp.int32, total.shape, 1)
    step = 1
    while step < BLOCK:
        total = total + jnp.where(lane >= step, pltpu.roll(total, step, 1), 0.0)
        step *= 2
    stage[0:HEADS, :] = total[0:HEADS, :]
    stage[HEADS : HEADS + 1, :] = doc.astype(jnp.float32)
    across = stage[...]
    return across, jnp.transpose(across)


def fetch(sources, targets, sems):
    copies = [pltpu.make_async_copy(s, t, sems.at[i]) for i, (s, t) in enumerate(zip(sources, targets))]
    for copy in copies:
        copy.start()
    return copies


def meta_of(log, last):
    row = lax.broadcasted_iota(jnp.int32, (16, HD), 0)
    high, middle, low = [part.astype(jnp.float32) for part in parts_of(log)]
    meta = jnp.where(row == 0, high, jnp.where(row == 1, middle, jnp.where(row == 2, low, 0.0)))
    return jnp.where(row == 3, last, meta).astype(jnp.bfloat16)


def read_meta(meta):
    meta = meta.astype(jnp.float32)
    return meta[0:1] + meta[1:2] + meta[2:3], meta[3:4]


def state_kernel(log_in, doc_in, key_in, value_in, weight_in, out_ref, log, doc, key, value, weight, stage, sems):
    copies = fetch(
        (log_in, doc_in, key_in, value_in, weight_in), (log, doc, key, value, weight), sems
    )
    copies[0].wait()
    copies[1].wait()
    _, down = running(log[...], doc[...], stage)
    final = down[BLOCK - 1 : BLOCK, :]
    kept = down[:, HEADS : HEADS + 1] == final[:, HEADS : HEADS + 1]
    to_end = jnp.where(kept, jnp.exp(final - down), 0.0)
    copies[2].wait()
    copies[3].wait()
    for h in range(HEADS):
        span = slice(h * HD, (h + 1) * HD)
        decayed = (key[:, span].astype(jnp.float32) * to_end[:, h : h + 1]).astype(jnp.bfloat16)
        state = dot(decayed, value[:, span], TN).astype(jnp.bfloat16)
        meta = meta_of(final[:, h : h + 1], final[:, HEADS : HEADS + 1])
        for half in range(2):
            out_ref[2 * h + half, 0:SLICE, :] = state[half * SLICE : (half + 1) * SLICE]
            out_ref[2 * h + half, SLICE:ROWS, :] = meta
    copies[4].wait()
    for k in range(RING):
        for j in range(4):
            out_ref[k, ROWS + 64 * j : ROWS + 64 * (j + 1), :] = weight[:, j * HD : (j + 1) * HD]


def row_kernel(states_ref, out_ref, weight_ref):
    total = jnp.zeros((SLICE, HD), jnp.float32)
    logs = jnp.zeros((1, HD), jnp.float32)
    prior = None
    for k in range(RING):
        log, last = read_meta(states_ref[k, SLICE:ROWS, :])
        if k:
            total = total * jnp.where(last == prior, jnp.exp(log), 0.0)
        total = total + states_ref[k, 0:SLICE, :].astype(jnp.float32)
        logs = logs + log
        prior = last
    for k in range(RING):
        out_ref[k, 0:SLICE, :] = total.astype(jnp.bfloat16)
        out_ref[k, SLICE:ROWS, :] = meta_of(logs, prior)
    weight_ref[...] = states_ref[:, ROWS:FULL, :]


def enter_kernel(states_ref, rows_ref, out_ref):
    here = lax.axis_index("y")
    entering = jnp.zeros((SLICE, HD), jnp.float32)
    memory = entering
    prior = jnp.zeros((1, HD), jnp.float32)
    prior_row = prior
    for k in range(RING):
        log, last = read_meta(rows_ref[k, SLICE:ROWS, :])
        memory = jnp.where(here == k, entering, memory)
        prior = jnp.where(here == k, prior_row, prior)
        entering = entering * jnp.where(last == prior_row, jnp.exp(log), 0.0)
        entering = entering + rows_ref[k, 0:SLICE, :].astype(jnp.float32)
        prior_row = last
    for k in range(RING):
        out_ref[k, 0:SLICE, :] = memory.astype(jnp.bfloat16)
        out_ref[k, SLICE:ROWS, :] = jnp.broadcast_to(prior, (16, HD)).astype(jnp.bfloat16)
        log, last = read_meta(states_ref[k, SLICE:ROWS, :])
        memory = memory * jnp.where(last == prior, jnp.exp(log), 0.0)
        memory = memory + states_ref[k, 0:SLICE, :].astype(jnp.float32)
        prior = last


def attend_kernel(
    log_in, doc_in, query_in, key_in, value_in, out_ref, across_ref,
    log, doc, query_ref, key_ref, value_ref, stage, mask, sems,
):
    copies = fetch(
        (log_in, doc_in, query_in, key_in, value_in), (log, doc, query_ref, key_ref, value_ref), sems
    )
    copies[0].wait()
    copies[1].wait()
    across, down = running(log[...], doc[...], stage)
    across_ref[...] = across
    doc_down = down[:, HEADS : HEADS + 1]
    row = lax.broadcasted_iota(jnp.int32, (BLOCK, BLOCK), 0)
    column = lax.broadcasted_iota(jnp.int32, (BLOCK, BLOCK), 1)
    seen = jnp.logical_and(row >= column, doc_down == across[HEADS : HEADS + 1, :])
    mask[...] = jnp.where(seen, 0.0, -1e30)
    part_rows = BLOCK // 2
    for copy in copies[2:]:
        copy.wait()
    for h in range(HEADS):
        span = slice(h * HD, (h + 1) * HD)
        for i in range(2):
            rows = slice(i * part_rows, (i + 1) * part_rows)
            seen = slice(0, (i + 1) * part_rows)
            scores = dot(query_ref[rows, span], key_ref[seen, span], NT)
            gap = down[rows, h : h + 1] - across[h : h + 1, seen] + mask[rows, seen]
            weighted = (scores * jnp.exp(gap)).astype(jnp.bfloat16)
            out_ref[rows, span] = dot(weighted, value_ref[seen, span]).astype(jnp.bfloat16)


def finish_kernel(across_ref, memory_ref, gain_ref, query_ref, local_ref, out_ref):
    across = across_ref[...]
    prior = memory_ref[0, SLICE : SLICE + 16, :].astype(jnp.float32)[0:1, 0:1]
    reach = jnp.transpose(jnp.where(across[HEADS : HEADS + 1, :] == prior, jnp.exp(across), 0.0))
    for h in range(HEADS):
        span = slice(h * HD, (h + 1) * HD)
        memory = jnp.concatenate([memory_ref[2 * h, 0:SLICE, :], memory_ref[2 * h + 1, 0:SLICE, :]], axis=0)
        heads = local_ref[:, span].astype(jnp.float32) + reach[:, h : h + 1] * dot(query_ref[:, span], memory)
        scale = lax.rsqrt(jnp.mean(heads * heads, axis=-1, keepdims=True) + 1e-06)
        out_ref[:, span] = (heads * scale * gain_ref[:, span]).astype(jnp.bfloat16)


def unpack(held, s):
    return jnp.concatenate(
        [held[s, :, 64 * j : 64 * (j + 1), :].reshape(BLOCK, HD) for j in range(4)], axis=1
    )


def half_kernel(block_ref, crossed_ref, out_ref):
    del crossed_ref
    out_ref[...] = block_ref[out_ref.shape[0] :, :]


def project_kernel(*refs):
    sources, (weight_in, out_ref, total, blocks, held, sems) = refs[:RING], refs[RING:]
    chips = lax.axis_size("x")
    x, c = lax.axis_index("x"), lax.axis_index("c")
    half = BLOCK // 2
    copies = []
    for s in range(RING):
        place = 2 * lax.rem(x + (0, -1, 1, 2)[s // 2] + chips, chips) + (1 - c if s % 2 else c)
        copies.append([pltpu.make_async_copy(weight_in.at[place], held.at[s], sems.at[s, 0])])
        copies[s].append(pltpu.make_async_copy(sources[s], blocks.at[s], sems.at[s, 1]))
        for copy in copies[s]:
            copy.start()
    for s in range(RING):
        for copy in copies[s]:
            copy.wait()
        for t in range(2):
            rows = slice(t * half, (t + 1) * half)
            product = dot(blocks[s, rows], unpack(held, s))
            if s == 0:
                total[rows] = product
            elif s < RING - 1:
                total[rows] += product
            else:
                out_ref[rows, :] = (total[rows] + product).astype(jnp.bfloat16)


def call(kernel, out_shape, args, specs, scratch=(), flops=0, transcendentals=0, grant=16):
    return pl.pallas_call(
        kernel,
        out_shape=out_shape,
        in_specs=specs,
        out_specs=jax.tree.map(lambda _: VMEM, out_shape),
        scratch_shapes=list(scratch),
        compiler_params=pltpu.CompilerParams(vmem_limit_bytes=grant * 2**20),
        cost_estimate=pl.CostEstimate(flops=flops, bytes_accessed=2**20, transcendentals=transcendentals),
    )(*args)


def local(sizes, queries, key_rows, value_rows, log_decay, doc_ids, head_gain, out_weight):
    nx = sizes[2]
    shape = lambda *dims: jax.ShapeDtypeStruct(dims, jnp.bfloat16)
    docs, gains = doc_ids.reshape(1, BLOCK), head_gain.reshape(1, -1)
    wide = pltpu.VMEM(queries.shape, jnp.bfloat16)
    logs_held = pltpu.VMEM(log_decay.shape, jnp.float32)
    docs_held = pltpu.VMEM(docs.shape, jnp.int32)
    stage = pltpu.VMEM((8, BLOCK), jnp.float32)

    states = call(
        state_kernel,
        shape(RING, FULL, HD),
        (log_decay, docs, key_rows, value_rows, out_weight),
        [ANY] * 5,
        [logs_held, docs_held, wide, wide, pltpu.VMEM(out_weight.shape, jnp.bfloat16), stage, pltpu.SemaphoreType.DMA((5,))],
        10**8,
        4096,
        GRANT,
    )
    states = lax.all_to_all(states, "z", 0, 0, tiled=True)
    rows, weight = call(
        row_kernel, (shape(RING, ROWS, HD), shape(RING, 256, HD)), (states,), [VMEM]
    )
    weight = lax.all_gather(weight, "y")
    rows = lax.all_to_all(rows, "y", 0, 0, tiled=True)
    entering = call(
        enter_kernel, shape(RING, ROWS, HD), (states, rows), [VMEM, VMEM]
    )
    entering = lax.all_to_all(entering, "z", 0, 0, tiled=True)

    alone, across = call(
        attend_kernel,
        (shape(*queries.shape), jax.ShapeDtypeStruct((8, BLOCK), jnp.float32)),
        (log_decay, docs, queries, key_rows, value_rows),
        [ANY] * 5,
        [logs_held, docs_held, wide, wide, wide, stage, pltpu.VMEM((BLOCK, BLOCK), jnp.float32)]
        + [pltpu.SemaphoreType.DMA((5,))],
        6 * 10**8,
        2**20,
        32,
    )
    normed = call(
        finish_kernel,
        shape(*queries.shape),
        (across, entering, gains, queries, alone),
        [VMEM] * 5,
        [],
        10**8,
        0,
        32,
    )

    right = [(i, (i + 1) % nx) for i in range(nx)]
    left = [(i, (i - 1) % nx) for i in range(nx)]
    before = lax.ppermute(normed, "x", right)
    after = lax.ppermute(normed, "x", left)
    half = BLOCK // 2
    crossed = lax.ppermute(normed, "c", [(0, 1), (1, 0)])
    last = call(half_kernel, shape(half, queries.shape[1]), (after, crossed), [VMEM, ANY])
    far_one = lax.ppermute(before[:half], "x", right)
    far_two = lax.ppermute(last, "x", left)
    cross = lambda block: lax.ppermute(block, "c", [(0, 1), (1, 0)])

    near = [normed, crossed, before, cross(before), after, cross(after)]
    far = jnp.concatenate([far_one, far_two])
    far = [far, cross(far)]
    return call(
        project_kernel,
        shape(*queries.shape),
        (*near, *far, weight),
        [ANY] * 9,
        [
            pltpu.VMEM(queries.shape, jnp.float32),
            pltpu.VMEM((RING, *queries.shape), jnp.bfloat16),
            pltpu.VMEM(weight.shape, jnp.bfloat16),
            pltpu.SemaphoreType.DMA((RING, 2)),
        ],
        2 * 10**9,
        0,
        58,
    )


def solution(mesh):
    sizes = (8, 8, 4, 2)
    split = Mesh(mesh.devices.reshape(sizes), ALL)
    ctx, tp = ("y", "z"), ("x", "c")
    return jax.shard_map(
        lambda *args: local(sizes, *args),
        mesh=split,
        in_specs=(P(ctx, tp), P(ctx, tp), P(ctx, tp), P(tp, ctx), P(ctx), P(tp), P(ctx, tp)),
        out_specs=P(ctx, tp),
        check_vma=False,
    )
```

```python
import jax
import jax.numpy as jnp
from jax import lax
from jax.experimental import pallas as pl
from jax.experimental.pallas import tpu as pltpu
from jax.sharding import Mesh, PartitionSpec as P

HD = 128
BLOCK = 512
HEADS = 4
RING = 8
SLICE = HEADS * HD // RING
ROWS = SLICE + 16
GRANT = 62
FULL = ROWS + 4 * 64
ALL = ("y", "z", "x", "c")
NT = (((1,), (1,)), ((), ()))
TN = (((0,), (0,)), ((), ()))
VMEM = pl.BlockSpec(memory_space=pltpu.VMEM)
ANY = pl.BlockSpec(memory_space=pl.ANY)
SMEM = pl.BlockSpec(memory_space=pltpu.SMEM)


def parts_of(value):
    high = value.astype(jnp.bfloat16)
    rest = value - high.astype(jnp.float32)
    middle = rest.astype(jnp.bfloat16)
    low = (rest - middle.astype(jnp.float32)).astype(jnp.bfloat16)
    return high, middle, low


def dot(a, b, dims=(((1,), (0,)), ((), ()))):
    return lax.dot_general(a, b, dims, preferred_element_type=jnp.float32)


def running(log, doc, stage):
    stage[...] = jnp.zeros_like(stage)
    stage[0:HEADS, :] = log
    total = stage[...]
    lane = lax.broadcasted_iota(jnp.int32, total.shape, 1)
    step = 1
    while step < BLOCK:
        total = total + jnp.where(lane >= step, pltpu.roll(total, step, 1), 0.0)
        step *= 2
    stage[0:HEADS, :] = total[0:HEADS, :]
    stage[HEADS : HEADS + 1, :] = doc.astype(jnp.float32)
    across = stage[...]
    return across, jnp.transpose(across)


def fetch(sources, targets, sems):
    copies = [pltpu.make_async_copy(s, t, sems.at[i]) for i, (s, t) in enumerate(zip(sources, targets))]
    for copy in copies:
        copy.start()
    return copies


def meta_of(log, last):
    row = lax.broadcasted_iota(jnp.int32, (16, HD), 0)
    high, middle, low = [part.astype(jnp.float32) for part in parts_of(log)]
    meta = jnp.where(row == 0, high, jnp.where(row == 1, middle, jnp.where(row == 2, low, 0.0)))
    return jnp.where(row == 3, last, meta).astype(jnp.bfloat16)


def read_meta(meta):
    meta = meta.astype(jnp.float32)
    return meta[0:1] + meta[1:2] + meta[2:3], meta[3:4]


def state_kernel(log_in, doc_in, key_in, value_in, weight_in, out_ref, log, doc, key, value, weight, stage, sems):
    copies = fetch(
        (log_in, doc_in, key_in, value_in, weight_in), (log, doc, key, value, weight), sems
    )
    copies[0].wait()
    copies[1].wait()
    _, down = running(log[...], doc[...], stage)
    final = down[BLOCK - 1 : BLOCK, :]
    kept = down[:, HEADS : HEADS + 1] == final[:, HEADS : HEADS + 1]
    to_end = jnp.where(kept, jnp.exp(final - down), 0.0)
    copies[2].wait()
    copies[3].wait()
    for h in range(HEADS):
        span = slice(h * HD, (h + 1) * HD)
        decayed = (key[:, span].astype(jnp.float32) * to_end[:, h : h + 1]).astype(jnp.bfloat16)
        state = dot(decayed, value[:, span], TN).astype(jnp.bfloat16)
        meta = meta_of(final[:, h : h + 1], final[:, HEADS : HEADS + 1])
        for half in range(2):
            out_ref[2 * h + half, 0:SLICE, :] = state[half * SLICE : (half + 1) * SLICE]
            out_ref[2 * h + half, SLICE:ROWS, :] = meta
    copies[4].wait()
    for k in range(RING):
        for j in range(4):
            out_ref[k, ROWS + 64 * j : ROWS + 64 * (j + 1), :] = weight[:, j * HD : (j + 1) * HD]


def row_kernel(states_ref, out_ref, weight_out, sems):
    (copy,) = fetch([states_ref.at[:, ROWS:FULL]], [weight_out], sems)
    total = jnp.zeros((SLICE, HD), jnp.float32)
    logs = jnp.zeros((1, HD), jnp.float32)
    prior = None
    for k in range(RING):
        log, last = read_meta(states_ref[k, SLICE:ROWS, :])
        if k:
            total = total * jnp.where(last == prior, jnp.exp(log), 0.0)
        total = total + states_ref[k, 0:SLICE, :].astype(jnp.float32)
        logs = logs + log
        prior = last
    for k in range(RING):
        out_ref[k, 0:SLICE, :] = total.astype(jnp.bfloat16)
        out_ref[k, SLICE:ROWS, :] = meta_of(logs, prior)
    copy.wait()


def enter_kernel(states_ref, rows_ref, out_ref):
    here = lax.axis_index("y")
    entering = jnp.zeros((SLICE, HD), jnp.float32)
    memory = entering
    prior = jnp.zeros((1, HD), jnp.float32)
    prior_row = prior
    for k in range(RING):
        log, last = read_meta(rows_ref[k, SLICE:ROWS, :])
        memory = jnp.where(here == k, entering, memory)
        prior = jnp.where(here == k, prior_row, prior)
        entering = entering * jnp.where(last == prior_row, jnp.exp(log), 0.0)
        entering = entering + rows_ref[k, 0:SLICE, :].astype(jnp.float32)
        prior_row = last
    for k in range(RING):
        out_ref[k, 0:SLICE, :] = memory.astype(jnp.bfloat16)
        out_ref[k, SLICE:ROWS, :] = jnp.broadcast_to(prior, (16, HD)).astype(jnp.bfloat16)
        log, last = read_meta(states_ref[k, SLICE:ROWS, :])
        memory = memory * jnp.where(last == prior, jnp.exp(log), 0.0)
        memory = memory + states_ref[k, 0:SLICE, :].astype(jnp.float32)
        prior = last


def attend_kernel(
    log_in, doc_in, query_in, key_in, value_in, out_ref, across_ref,
    log, doc, query_ref, key_ref, value_ref, stage, mask, sems,
):
    copies = fetch(
        (log_in, doc_in, query_in, key_in, value_in), (log, doc, query_ref, key_ref, value_ref), sems
    )
    copies[0].wait()
    copies[1].wait()
    across, down = running(log[...], doc[...], stage)
    across_ref[...] = across
    doc_down = down[:, HEADS : HEADS + 1]
    row = lax.broadcasted_iota(jnp.int32, (BLOCK, BLOCK), 0)
    column = lax.broadcasted_iota(jnp.int32, (BLOCK, BLOCK), 1)
    seen = jnp.logical_and(row >= column, doc_down == across[HEADS : HEADS + 1, :])
    mask[...] = jnp.where(seen, 0.0, -1e30)
    part_rows = BLOCK // 2
    for copy in copies[2:]:
        copy.wait()
    for h in range(HEADS):
        span = slice(h * HD, (h + 1) * HD)
        for i in range(2):
            rows = slice(i * part_rows, (i + 1) * part_rows)
            seen = slice(0, (i + 1) * part_rows)
            scores = dot(query_ref[rows, span], key_ref[seen, span], NT)
            gap = down[rows, h : h + 1] - across[h : h + 1, seen] + mask[rows, seen]
            weighted = (scores * jnp.exp(gap)).astype(jnp.bfloat16)
            out_ref[rows, span] = dot(weighted, value_ref[seen, span]).astype(jnp.bfloat16)


def finish_kernel(across_ref, memory_ref, gain_ref, query_ref, local_ref, out_ref):
    across = across_ref[...]
    prior = memory_ref[0, SLICE : SLICE + 16, :].astype(jnp.float32)[0:1, 0:1]
    reach = jnp.transpose(jnp.where(across[HEADS : HEADS + 1, :] == prior, jnp.exp(across), 0.0))
    for h in range(HEADS):
        span = slice(h * HD, (h + 1) * HD)
        memory = jnp.concatenate([memory_ref[2 * h, 0:SLICE, :], memory_ref[2 * h + 1, 0:SLICE, :]], axis=0)
        heads = local_ref[:, span].astype(jnp.float32) + reach[:, h : h + 1] * dot(query_ref[:, span], memory)
        scale = lax.rsqrt(jnp.mean(heads * heads, axis=-1, keepdims=True) + 1e-06)
        out_ref[:, span] = (heads * scale * gain_ref[:, span]).astype(jnp.bfloat16)


def unpack(held, s):
    return jnp.concatenate(
        [held[s, :, 64 * j : 64 * (j + 1), :].reshape(BLOCK, HD) for j in range(4)], axis=1
    )


def half_kernel(block_ref, crossed_ref, out_ref):
    del crossed_ref
    out_ref[...] = block_ref[out_ref.shape[0] :, :]


def project_kernel(*refs):
    sources, (weight_in, out_ref, total, blocks, held, sems) = refs[:RING], refs[RING:]
    chips = lax.axis_size("x")
    x, c = lax.axis_index("x"), lax.axis_index("c")
    half = BLOCK // 2
    copies = []
    for s in range(RING):
        place = 2 * lax.rem(x + (0, -1, 1, 2)[s // 2] + chips, chips) + (1 - c if s % 2 else c)
        copies.append([pltpu.make_async_copy(weight_in.at[place], held.at[s], sems.at[s, 0])])
        copies[s].append(pltpu.make_async_copy(sources[s], blocks.at[s], sems.at[s, 1]))
        for copy in copies[s]:
            copy.start()
    for s in range(RING):
        for copy in copies[s]:
            copy.wait()
        for t in range(2):
            rows = slice(t * half, (t + 1) * half)
            product = dot(blocks[s, rows], unpack(held, s))
            if s == 0:
                total[rows] = product
            elif s < RING - 1:
                total[rows] += product
            else:
                out_ref[rows, :] = (total[rows] + product).astype(jnp.bfloat16)


def call(kernel, out_shape, args, specs, scratch=(), flops=0, transcendentals=0, grant=16, outs=None):
    return pl.pallas_call(
        kernel,
        out_shape=out_shape,
        in_specs=specs,
        out_specs=outs or jax.tree.map(lambda _: VMEM, out_shape),
        scratch_shapes=list(scratch),
        compiler_params=pltpu.CompilerParams(vmem_limit_bytes=grant * 2**20),
        cost_estimate=pl.CostEstimate(flops=flops, bytes_accessed=2**20, transcendentals=transcendentals),
    )(*args)


def local(sizes, queries, key_rows, value_rows, log_decay, doc_ids, head_gain, out_weight):
    nx = sizes[2]
    shape = lambda *dims: jax.ShapeDtypeStruct(dims, jnp.bfloat16)
    docs, gains = doc_ids.reshape(1, BLOCK), head_gain.reshape(1, -1)
    wide = pltpu.VMEM(queries.shape, jnp.bfloat16)
    logs_held = pltpu.VMEM(log_decay.shape, jnp.float32)
    docs_held = pltpu.VMEM(docs.shape, jnp.int32)
    stage = pltpu.VMEM((8, BLOCK), jnp.float32)

    states = call(
        state_kernel,
        shape(RING, FULL, HD),
        (log_decay, docs, key_rows, value_rows, out_weight),
        [ANY] * 5,
        [logs_held, docs_held, wide, wide, pltpu.VMEM(out_weight.shape, jnp.bfloat16), stage, pltpu.SemaphoreType.DMA((5,))],
        10**8,
        4096,
        GRANT,
    )
    states = lax.all_to_all(states, "z", 0, 0, tiled=True)
    rows, weight = call(
        row_kernel,
        (shape(RING, ROWS, HD), shape(RING, 256, HD)),
        (states,),
        [VMEM],
        [pltpu.SemaphoreType.DMA((1,))],
        outs=[VMEM, ANY],
    )
    weight = lax.all_gather(weight, "y")
    rows = lax.all_to_all(rows, "y", 0, 0, tiled=True)
    entering = call(
        enter_kernel, shape(RING, ROWS, HD), (states, rows), [VMEM, VMEM]
    )
    entering = lax.all_to_all(entering, "z", 0, 0, tiled=True)

    alone, across = call(
        attend_kernel,
        (shape(*queries.shape), jax.ShapeDtypeStruct((8, BLOCK), jnp.float32)),
        (log_decay, docs, queries, key_rows, value_rows),
        [ANY] * 5,
        [logs_held, docs_held, wide, wide, wide, stage, pltpu.VMEM((BLOCK, BLOCK), jnp.float32)]
        + [pltpu.SemaphoreType.DMA((5,))],
        6 * 10**8,
        2**20,
        32,
    )
    normed = call(
        finish_kernel,
        shape(*queries.shape),
        (across, entering, gains, queries, alone),
        [VMEM] * 5,
        [],
        10**8,
        0,
        32,
    )

    right = [(i, (i + 1) % nx) for i in range(nx)]
    left = [(i, (i - 1) % nx) for i in range(nx)]
    before = lax.ppermute(normed, "x", right)
    after = lax.ppermute(normed, "x", left)
    half = BLOCK // 2
    crossed = lax.ppermute(normed, "c", [(0, 1), (1, 0)])
    last = call(half_kernel, shape(half, queries.shape[1]), (after, crossed), [VMEM, ANY])
    far_one = lax.ppermute(before[:half], "x", right)
    far_two = lax.ppermute(last, "x", left)
    cross = lambda block: lax.ppermute(block, "c", [(0, 1), (1, 0)])

    near = [normed, crossed, before, cross(before), after, cross(after)]
    far = jnp.concatenate([far_one, far_two])
    far = [far, cross(far)]
    return call(
        project_kernel,
        shape(*queries.shape),
        (*near, *far, weight),
        [ANY] * 9,
        [
            pltpu.VMEM(queries.shape, jnp.float32),
            pltpu.VMEM((RING, *queries.shape), jnp.bfloat16),
            pltpu.VMEM(weight.shape, jnp.bfloat16),
            pltpu.SemaphoreType.DMA((RING, 2)),
        ],
        2 * 10**9,
        0,
        58,
    )


def solution(mesh):
    sizes = (8, 8, 4, 2)
    split = Mesh(mesh.devices.reshape(sizes), ALL)
    ctx, tp = ("y", "z"), ("x", "c")
    return jax.shard_map(
        lambda *args: local(sizes, *args),
        mesh=split,
        in_specs=(P(ctx, tp), P(ctx, tp), P(ctx, tp), P(tp, ctx), P(ctx), P(tp), P(ctx, tp)),
        out_specs=P(ctx, tp),
        check_vma=False,
    )
```
